512 devices in a mesh: table: 32 (over z, core), ctx: 16 (over y, x).
Axes of the slice: x: 4, y: 4, z: 16, core: 2. Of those that a mesh axis runs over, the one named last changes fastest.
Arguments:
- item_ids: int32 [32, 2048], P('table', 'ctx'), may hold values from 0 to 16383, as said below
- history_len: int32 [32], P('table'), may hold values from 1 to 2048, 40960 in all
- item_slot: int32 [16384], replicated, may hold values from 0 to 16383, as said below
- table_slab: float32 [16384, 512], P('table'), may hold values from -20 to 20
- proj_in: bfloat16 [512, 2048], replicated, may hold values from -0.25 to 0.25
- proj_out: bfloat16 [512, 512], replicated, may hold values from -0.25 to 0.25
- upstream: bfloat16 [32, 2048, 512], P('table', 'ctx'), may hold values from -6 to 6
Outputs:
- layer_out: bfloat16 [32, 2048, 512], P('table', 'ctx')
- table_grad: float32 [16384, 512], P(('table', 'ctx'))
The draws below stay inside these ranges and needn't reach their ends.
Inputs may be any that keep to these rules, and one draw needn't show every extreme that they name: `item_slot`: A permutation of the slots; slot s is row s % 512 of table shard s // 512. `item_ids`: in each aligned block of 128 event slots of one history (the events of one device), at most 12 items have their slot on any one table shard, and exactly 12 on some shard.
All inputs are finite; a program needn't handle non-finite values. No bound on the sum of `history_len` on one device may be relied on, other than what follows from the above.
Results may differ from the reference program's by a relative error of at most 0.013.
Values may be sent and summed in bfloat16 or wider, within the bound.
No kernel may reach another device: no remote copies, remote signals or barrier semaphores. Data moves between devices by JAX's collectives and lax.ppermute only.
A program may use at most 128 MiB of HBM per device.

```python
import math
import jax
import jax.numpy as jnp
import numpy as np
from jax import lax

D = 512
HEADS = 4
HEAD_DIM = 128
ATT = 512
BLK = 128
L = 2048
USERS = 32
ROWS_DEV = 512
ROWS = 16384
CAP = 12


def slot_order(key):
    return jax.random.permutation(key, ROWS).astype(jnp.int32)


def draw_item_slot(key, part):
    return slot_order(key)


def draw_item_ids(key, part):
    slot_of_item = slot_order(key)
    item_of_slot = jnp.argsort(slot_of_item, stable=True).astype(jnp.int32)
    key = jax.random.fold_in(key, 3)
    key_hot, key_shuffle, key_rows = jax.random.split(key, 3)
    blocks = USERS * (L // BLK)
    hottest = jax.random.randint(key_hot, (blocks,), 0, USERS)
    places = jnp.arange(BLK)
    offsets = jnp.where(places < CAP, 0, 1 + (places - CAP) % (USERS - 1))
    owners = (hottest[:, None] + offsets[None, :]) % USERS
    shuffles = jax.vmap(lambda one_key: jax.random.permutation(one_key, BLK))(jax.random.split(key_shuffle, blocks))
    owners = jnp.take_along_axis(owners, shuffles, axis=1)
    local_rows = jax.random.randint(key_rows, (blocks, BLK), 0, ROWS_DEV)
    slots = owners * ROWS_DEV + local_rows
    return item_of_slot[slots].reshape(USERS, L).astype(jnp.int32)


def draw_table_slab(key, part):
    key = jax.random.fold_in(key, 7)
    key_base, key_rows, key_cols = jax.random.split(key, 3)
    base = jnp.clip(jax.random.normal(key_base, (ROWS, D), jnp.float32), -4.0, 4.0)
    row_scale = jnp.exp(jax.random.uniform(key_rows, (ROWS, 1), jnp.float32, -1.15, 1.15))
    col_scale = jnp.exp(jax.random.uniform(key_cols, (1, D), jnp.float32, -1.15, 1.15))
    return 0.5 * base * row_scale * col_scale


def steps_of(key, extent, cuts, smallest, top_value):
    def one(dim, parts):
        heights = jax.random.uniform(jax.random.fold_in(jax.random.fold_in(key, 6), dim), (parts,), jnp.float32, smallest / len(cuts), top_value / len(cuts))
        return jnp.repeat(jnp.exp(heights), extent[dim] // parts).reshape((-1,) + (1,) * (len(extent) - dim - 1))

    level = one(*cuts[0])
    for cut in cuts[1:]:
        level = level * one(*cut)
    return level


def profile(number_of, total, bound, lean):
    loads = [(1 << 20) // math.isqrt(grade ** lean) + 1 for grade in range(2, number_of + 1)]
    rest, given = total - bound - (number_of - 1), [1] * (number_of - 1)
    while rest > 0:
        movable = [i for i in range(number_of - 1) if given[i] < bound]
        pool, remaining = sum([loads[i] for i in movable]), rest
        for i in movable:
            more = min(bound - given[i], max(1, remaining * loads[i] // pool), rest)
            given[i] = given[i] + more
            rest = rest - more
    return np.array([bound] + given)


def uneven(key, amount, total, limit, slope):
    if amount == 2:
        one = jax.random.randint(key, (), max(1, total - limit), min(limit, total - 1) + 1)
        return jnp.stack([one, total - one])
    sizes = jnp.asarray(profile(amount, total, limit, slope), jnp.int32)
    twos = (amount - 1) // 2
    donor, taker = sizes[1:1 + 2 * twos:2], sizes[2:2 + 2 * twos:2]
    margin = jnp.minimum(donor - 1, limit - taker)
    passed = jax.random.randint(jax.random.fold_in(key, 1), (twos,), 0, 1 << 20) % (margin + 1)
    sizes = sizes.at[1:1 + 2 * twos:2].set(donor - passed).at[2:2 + 2 * twos:2].set(taker + passed)
    return sizes[jax.random.permutation(jax.random.fold_in(key, 2), amount)]


def scatter_about(key, shape, deviation, limit, cuts=(), kind=jnp.bfloat16):
    level = steps_of(key, shape, cuts, -0.22, 0.18) if cuts else 1.0
    result = jax.random.normal(key, shape, jnp.float32) * deviation * level
    return jnp.minimum(jnp.maximum(result, -limit), limit).astype(kind)


def setup_inputs(seed: int = 0) -> dict:
    splits = jax.random.split(jax.random.key(seed), 8)
    return {
        "item_ids": draw_item_ids(jax.random.fold_in(splits[7], 71), 0),
        "history_len": uneven(splits[1], USERS, USERS * L * 5 // 8, L, 2).astype(jnp.int32),
        "item_slot": draw_item_slot(jax.random.fold_in(splits[7], 71), 0),
        "table_slab": draw_table_slab(jax.random.fold_in(splits[7], 71), 0),
        "proj_in": scatter_about(splits[4], (D, 4 * ATT), D ** -0.5, 0.25),
        "proj_out": scatter_about(splits[5], (ATT, D), ATT ** -0.5, 0.25),
        "upstream": scatter_about(splits[6], (USERS, L, D), 1.0, 6.0, ((0, 32), (1, 16))),
    }


EPSILON = 1e-05

def normalize(values):
    centre = values - lax.optimization_barrier(jnp.mean(values, axis=-1, keepdims=True))
    scale_inv = lax.rsqrt(lax.optimization_barrier(jnp.mean(centre * centre, axis=-1, keepdims=True)) + EPSILON)
    return (centre * scale_inv, scale_inv)

def norm_back(grad, normed, scale_inv):
    return scale_inv * (grad - lax.optimization_barrier(jnp.mean(grad, axis=-1, keepdims=True)) - normed * lax.optimization_barrier(jnp.mean(grad * normed, axis=-1, keepdims=True)))

def silu_slope(values):
    sig = jax.nn.sigmoid(values)
    return sig * (1.0 + values * (1.0 - sig))

def reference(item_ids, history_len, item_slot, table_slab, proj_in, proj_out, upstream):
    score_scale = HEAD_DIM ** (-0.5)

    def one_user(packed):
        user_ids, length, user_grad = packed
        slots = item_slot[user_ids]
        positions = jnp.arange(L).astype(jnp.int32)
        validity = (positions < length).astype(jnp.float32)
        embedded = table_slab[slots] * validity[:, None]
        normed, inv_std = normalize(embedded)
        projected = jnp.dot(normed.astype(jnp.bfloat16), proj_in, preferred_element_type=jnp.float32)
        gate_part = projected[:, :2 * ATT]
        features = jnp.concatenate([jax.nn.silu(gate_part), projected[:, 2 * ATT:]], axis=1).astype(jnp.bfloat16)
        gate_u = features[:, :ATT].astype(jnp.float32)
        value_heads = features[:, ATT:2 * ATT].astype(jnp.float32).reshape(L, HEADS, HEAD_DIM)
        query_heads = features[:, 2 * ATT:3 * ATT].astype(jnp.float32).reshape(L, HEADS, HEAD_DIM)
        key_heads = features[:, 3 * ATT:].astype(jnp.float32).reshape(L, HEADS, HEAD_DIM)
        allowed = ((positions[None, :] <= positions[:, None]) & (positions[None, :] < length)).astype(jnp.float32)
        scores = jnp.einsum('qhd,khd->hqk', query_heads, key_heads) * score_scale
        weights = (jax.nn.silu(scores) * allowed[None]).astype(jnp.bfloat16)
        weights_wide = weights.astype(jnp.float32)
        attended = jnp.einsum('hqk,khd->qhd', weights_wide, value_heads).reshape(L, ATT)
        att_hat, att_inv = normalize(attended)
        gated = (att_hat * gate_u).astype(jnp.bfloat16)
        layer_out = ((embedded + jnp.dot(gated, proj_out, preferred_element_type=jnp.float32)) * validity[:, None]).astype(jnp.bfloat16)
        d_out = user_grad * validity[:, None].astype(jnp.bfloat16)
        d_gated = jnp.dot(d_out, proj_out.T, preferred_element_type=jnp.float32)
        d_gate = d_gated * att_hat
        d_attn = norm_back(d_gated * gate_u, att_hat, att_inv).astype(jnp.bfloat16)
        d_heads = d_attn.astype(jnp.float32).reshape(L, HEADS, HEAD_DIM)
        d_weights = jnp.einsum('qhd,khd->hqk', d_heads, value_heads)
        d_scores = (d_weights * silu_slope(scores) * allowed[None] * score_scale).astype(jnp.bfloat16).astype(jnp.float32)
        d_query = jnp.einsum('hqk,khd->qhd', d_scores, key_heads).reshape(L, ATT)
        d_key = jnp.einsum('hqk,qhd->khd', d_scores, query_heads).reshape(L, ATT)
        d_value = jnp.einsum('hqk,qhd->khd', weights_wide, d_heads).reshape(L, ATT)
        d_proj = jnp.concatenate([jnp.concatenate([d_gate, d_value], axis=1) * silu_slope(gate_part), d_query, d_key], axis=1).astype(jnp.bfloat16)
        d_normed = jnp.dot(d_proj, proj_in.T, preferred_element_type=jnp.float32)
        d_embedded = (d_out.astype(jnp.float32) + norm_back(d_normed, normed, inv_std)) * validity[:, None]
        return (layer_out, slots, d_embedded)
    layer_out, slots, grads = lax.map(one_user, (item_ids, history_len, upstream))
    table_grad = jnp.zeros((ROWS, D), jnp.float32).at[slots.reshape(-1)].add(grads.reshape(-1, D))
    return (layer_out, table_grad)
```

```python
import jax
import jax.numpy as jnp
from jax import lax
from jax.experimental import pallas as pl
from jax.experimental.pallas import tpu as pltpu
from jax.sharding import PartitionSpec as P

EPSILON = 1e-05
BLOCK = 128
WIDTH = 512
HEADS = 4
HEAD_DIM = 128
TABLES = 32
GROUPS = 16
SHARD_ROWS = 512
QUERIES = BLOCK // HEADS
SEQ = BLOCK * GROUPS
SPAN = 4 * BLOCK
SCALE = HEAD_DIM ** (-0.5)
PIECE = 2 * BLOCK + 2 * QUERIES
MAIN = 8
SENT = TABLES * MAIN
PACKED = WIDTH + WIDTH // 2

F32 = jnp.float32
BF16 = jnp.bfloat16


def dot(a, b):
    return jnp.dot(a, b, preferred_element_type=F32)


def dot_nt(a, b):
    return lax.dot_general(a, b, (((1,), (1,)), ((), ())), preferred_element_type=F32)


def dot_tn(a, b):
    return lax.dot_general(a, b, (((0,), (0,)), ((), ())), preferred_element_type=F32)


def iota(shape, dim):
    return lax.broadcasted_iota(jnp.int32, shape, dim)


def one_hot(mask):
    return jnp.where(mask, 1.0, 0.0).astype(BF16)


def normalize(values):
    centre = values - jnp.mean(values, axis=-1, keepdims=True)
    scale_inv = lax.rsqrt(jnp.mean(centre * centre, axis=-1, keepdims=True) + EPSILON)
    return (centre * scale_inv, scale_inv)


def norm_back(grad, normed, scale_inv):
    return scale_inv * (
        grad
        - jnp.mean(grad, axis=-1, keepdims=True)
        - normed * jnp.mean(grad * normed, axis=-1, keepdims=True)
    )


def index_kernel(length_ref, ids_ref, slot_ref, send_ref, info_ref):
    ids = ids_ref[...]
    event = iota((1, BLOCK), 1)
    valid = lax.axis_index("ctx") * BLOCK + event < length_ref[0]
    row = iota((BLOCK, BLOCK), 0)
    table = slot_ref[...]
    rows_hot = one_hot(row == (ids >> 7))
    high = dot_tn((table >> 7).astype(F32).astype(BF16), rows_hot)
    low = dot_tn((table & 127).astype(F32).astype(BF16), rows_hot)
    both = jnp.where(row == (ids & 127), high * 128.0 + low, 0.0)
    slots = jnp.sum(both, axis=0, keepdims=True).astype(jnp.int32)
    owner = jnp.where(valid, slots >> 9, TABLES)
    wanted = (slots & (SHARD_ROWS - 1)) + 1
    owned = iota((TABLES, BLOCK), 0) == owner
    earlier = dot(one_hot(owned), one_hot(row < iota((BLOCK, BLOCK), 1)))
    rank = jnp.sum(jnp.where(owned, earlier, 0.0), axis=0, keepdims=True).astype(jnp.int32)
    head = jnp.where(valid & (rank < MAIN), owner * MAIN + rank, -1000)
    tail = jnp.where(valid & (rank >= MAIN), owner * MAIN + rank - MAIN, -1000)
    info_ref[...] = jnp.concatenate([head, tail, head, tail, head, tail, head, tail], axis=0)
    place = iota((SENT, BLOCK), 0)
    in_head = one_hot(place == head)
    in_tail = one_hot((place == tail) | (place == tail + 4))
    wide = jnp.broadcast_to(wanted, (BLOCK, BLOCK))
    wide_high = (wide >> 5).astype(F32).astype(BF16)
    wide_low = (wide & 31).astype(F32).astype(BF16)
    ask_head = dot_nt(in_head, wide_high) * 32.0 + dot_nt(in_head, wide_low)
    ask_tail = dot_nt(in_tail, wide_high) * 32.0 + dot_nt(in_tail, wide_low)
    asked = jnp.where(iota((SENT, BLOCK), 1) < BLOCK // 2, ask_head, ask_tail)
    send_ref[...] = asked.astype(jnp.int32)


def spread(asked):
    turned = pltpu.roll(asked, BLOCK // 2, 1)
    left = iota((SENT, BLOCK), 1) < BLOCK // 2
    return jnp.where(left, asked, turned), jnp.where(left, turned, asked)


def gather_kernel(asked_ref, slab_ref, out_ref):
    head, tail = spread(asked_ref[...])
    column = iota((SENT, BLOCK), 1) + 1
    spans = [column + BLOCK * k for k in range(SHARD_ROWS // BLOCK)]
    slab = slab_ref[...].astype(BF16)
    hot_head = jnp.concatenate([one_hot(head == span) for span in spans], axis=1)
    hot_tail = jnp.concatenate([one_hot(tail == span) for span in spans], axis=1)
    out_ref[:, :WIDTH] = dot(hot_head, slab).astype(BF16)
    rest = dot(hot_tail, slab)
    half = WIDTH // 2
    first = (iota((SENT, half), 0) & 7) < 4
    out_ref[:, WIDTH:] = jnp.where(first, rest[:, :half], rest[:, half:]).astype(BF16)


def cotangent_kernel(length_ref, upstream_ref, proj_out_ref, d_gated_ref):
    place = lax.axis_index("ctx") * BLOCK + iota((BLOCK, WIDTH), 0)
    d_out = jnp.where(place < length_ref[0], upstream_ref[...], jnp.zeros((), BF16))
    d_gated_ref[...] = dot_nt(d_out, proj_out_ref[...])


def place_masks(info_ref):
    place = iota((SENT, BLOCK), 0)
    head, tail = info_ref[0:1, :], info_ref[1:2, :]
    return one_hot(place == head), one_hot(place == tail), one_hot(place == tail + 4)


def project_kernel(
    info_ref, rows_ref, proj_in_ref, d_gated_ref, send_ref, embedded_ref, gate_ref, slope_ref
):
    in_head, in_first, in_second = place_masks(info_ref)
    half = WIDTH // 2
    rest = rows_ref[:, WIDTH:]
    embedded = dot_tn(in_head, rows_ref[:, :WIDTH]) + jnp.concatenate(
        [dot_tn(in_first, rest), dot_tn(in_second, rest)], axis=1
    )
    embedded_ref[...] = embedded.astype(BF16)
    normed = normalize(embedded)[0].astype(BF16)

    def part(k):
        return dot(normed, proj_in_ref[:, k * WIDTH : (k + 1) * WIDTH])

    def silu(values):
        sig = jax.nn.sigmoid(values)
        return values * sig, sig * (1.0 + values * (1.0 - sig))

    gate, slope_gate = silu(part(0))
    value, slope_value = silu(part(1))
    slope_ref[:, :WIDTH] = slope_gate
    slope_ref[:, WIDTH:] = slope_value
    gate = gate.astype(BF16)
    gate_ref[...] = gate
    value = value.astype(BF16)
    query = part(2).astype(BF16)
    key = part(3).astype(BF16)
    d_hat = (d_gated_ref[...] * gate.astype(F32)).astype(BF16)
    for h in range(HEADS):
        cols = slice(h * HEAD_DIM, (h + 1) * HEAD_DIM)
        for g in range(HEADS):
            rows = slice(g * QUERIES, (g + 1) * QUERIES)
            chunk = HEADS * g + h
            send_ref[chunk, 0:BLOCK, :] = key[:, cols]
            send_ref[chunk, BLOCK : 2 * BLOCK, :] = value[:, cols]
            send_ref[chunk, 2 * BLOCK : 2 * BLOCK + QUERIES, :] = query[rows, cols]
            send_ref[chunk, 2 * BLOCK + QUERIES :, :] = d_hat[rows, cols]


def allowed_mask():
    group = lax.axis_index("ctx") // HEADS
    lane = iota((SPAN, BLOCK), 1)
    place = (lane // QUERIES) * BLOCK + group * QUERIES + lane % QUERIES
    return iota((SPAN, BLOCK), 0) <= place


def span_keys(recv_ref, j):
    chunks = slice(4 * j, 4 * j + 4)
    key = recv_ref[chunks, 0:BLOCK, :].reshape(SPAN, HEAD_DIM)
    value = recv_ref[chunks, BLOCK : 2 * BLOCK, :].reshape(SPAN, HEAD_DIM)
    return key, value


def attend_kernel(recv_ref, att_ref, d_hat_ref, stats_ref):
    query = recv_ref[:, 2 * BLOCK : 2 * BLOCK + QUERIES, :].reshape(SPAN, HEAD_DIM)
    mask = allowed_mask()
    for j in range(4):
        key, value = span_keys(recv_ref, j)
        start = j * BLOCK
        half = dot_nt(key, query[start:, :]) * (0.5 * SCALE)
        weight = half + half * jnp.tanh(half)
        weight = jnp.concatenate(
            [jnp.where(mask, weight[:, :BLOCK], 0.0), weight[:, BLOCK:]], axis=1
        ) if j < 3 else jnp.where(mask, weight, 0.0)
        part = dot_tn(value, weight.astype(BF16))
        if j == 0:
            att_ref[...] = part
        else:
            att_ref[:, start:] += part
    d_hat = recv_ref[:, 2 * BLOCK + QUERIES :, :].reshape(SPAN, HEAD_DIM)
    d_hat = d_hat.astype(F32).T
    d_hat_ref[...] = d_hat
    att = att_ref[...]
    mean = jnp.mean(att, axis=0, keepdims=True)
    centre = att - mean
    d_mean = jnp.mean(d_hat, axis=0, keepdims=True)
    spread_sum = jnp.sum(centre * centre, axis=0, keepdims=True)
    cross_sum = jnp.sum(centre * (d_hat - d_mean), axis=0, keepdims=True)
    rows = jnp.concatenate(
        [mean, spread_sum, d_mean, cross_sum, mean, spread_sum, d_mean, cross_sum], axis=0
    )
    for k in range(HEADS):
        stats_ref[k] = rows


def backward_kernel(recv_ref, att_ref, d_hat_ref, stats_ref, send_ref, d_query_ref):
    query = recv_ref[:, 2 * BLOCK : 2 * BLOCK + QUERIES, :].reshape(SPAN, HEAD_DIM)
    mask = allowed_mask()
    stats = [stats_ref[k] for k in range(HEADS)]

    def average(row):
        return sum(s[row : row + 1, :] for s in stats) / HEADS

    mean, d_mean = average(0), average(2)
    spread_mean = average(1) / HEAD_DIM + sum(
        (s[0:1, :] - mean) * (s[0:1, :] - mean) for s in stats
    ) / HEADS
    cross_mean = average(3) / HEAD_DIM + sum(
        (s[0:1, :] - mean) * (s[2:3, :] - d_mean) for s in stats
    ) / HEADS
    inv = lax.rsqrt(spread_mean + EPSILON)
    att = att_ref[...]
    att_hat = (att - mean) * inv
    d_att = (inv * (d_hat_ref[...] - d_mean - att_hat * (inv * cross_mean))).astype(BF16)
    out_att = att.T.astype(BF16)
    for j in range(4):
        key, value = span_keys(recv_ref, j)
        start = j * BLOCK
        half = dot_nt(key, query[start:, :]) * (0.5 * SCALE)
        th = jnp.tanh(half)
        weight = half + half * th
        slope = (0.5 * SCALE) * ((1.0 + th) + weight * (1.0 - th))
        d_score = dot(value, d_att[:, start:]) * slope

        def masked(values):
            first = jnp.where(mask, values[:, :BLOCK], 0.0)
            if j == 3:
                return first.astype(BF16)
            return jnp.concatenate([first, values[:, BLOCK:]], axis=1).astype(BF16)

        weight, d_score = masked(weight), masked(d_score)
        d_key = dot(d_score, query[start:, :]).astype(BF16)
        d_value = dot_nt(weight, d_att[:, start:]).astype(BF16)
        part = dot_tn(key, d_score)
        if j == 0:
            d_query_ref[...] = part
        else:
            d_query_ref[:, start:] += part
        for k in range(4):
            rows = slice(k * BLOCK, (k + 1) * BLOCK)
            send_ref[4 * j + k, 0:BLOCK, :] = d_key[rows]
            send_ref[4 * j + k, BLOCK : 2 * BLOCK, :] = d_value[rows]
    d_query = d_query_ref[...].T.astype(BF16)
    for c in range(GROUPS):
        rows = slice(c * QUERIES, (c + 1) * QUERIES)
        send_ref[c, 2 * BLOCK : 2 * BLOCK + QUERIES, :] = d_query[rows]
        send_ref[c, 2 * BLOCK + QUERIES :, :] = out_att[rows]


def collect(recv_ref, first, rows):
    return jnp.concatenate(
        [
            jnp.concatenate([recv_ref[HEADS * g + h, first : first + rows, :] for g in range(HEADS)], axis=0)
            for h in range(HEADS)
        ],
        axis=1,
    ).astype(F32)


def collect_sum(recv_ref, first):
    def head(h):
        return sum(
            recv_ref[HEADS * g + h, first : first + BLOCK, :].astype(F32) for g in range(HEADS)
        )

    return jnp.concatenate([head(h) for h in range(HEADS)], axis=1)


def finish_kernel(
    length_ref,
    info_ref,
    recv_ref,
    embedded_ref,
    slope_ref,
    d_gated_ref,
    upstream_ref,
    proj_in_ref,
    out_ref,
    att_hat_ref,
):
    att_hat = normalize(collect(recv_ref, 2 * BLOCK + QUERIES, QUERIES))[0]
    att_hat_ref[...] = att_hat
    d_value = collect_sum(recv_ref, BLOCK) * slope_ref[:, WIDTH:]
    d_gate = d_gated_ref[...] * att_hat * slope_ref[:, :WIDTH]
    d_query = collect(recv_ref, 2 * BLOCK, QUERIES)
    d_key = collect_sum(recv_ref, 0)
    d_normed = jnp.zeros((BLOCK, WIDTH), F32)
    for k, part in enumerate((d_gate, d_value, d_query, d_key)):
        d_normed += dot_nt(part.astype(BF16), proj_in_ref[:, k * WIDTH : (k + 1) * WIDTH])
    normed, inv_std = normalize(embedded_ref[...].astype(F32))
    place = lax.axis_index("ctx") * BLOCK + iota((BLOCK, WIDTH), 0)
    d_embedded = jnp.where(
        place < length_ref[0],
        upstream_ref[...].astype(F32) + norm_back(d_normed, normed, inv_std),
        0.0,
    ).astype(BF16)
    in_head, in_first, in_second = place_masks(info_ref)
    half = WIDTH // 2
    out_ref[:, :WIDTH] = dot(in_head, d_embedded).astype(BF16)
    out_ref[:, WIDTH:] = (
        dot(in_first, d_embedded[:, :half]) + dot(in_second, d_embedded[:, half:])
    ).astype(BF16)


def output_kernel(length_ref, att_hat_ref, gate_ref, embedded_ref, proj_out_ref, out_ref):
    gated = (att_hat_ref[...] * gate_ref[...].astype(F32)).astype(BF16)
    total = embedded_ref[...].astype(F32) + dot(gated, proj_out_ref[...])
    place = lax.axis_index("ctx") * BLOCK + iota((BLOCK, WIDTH), 0)
    out_ref[...] = jnp.where(place < length_ref[0], total, 0.0).astype(BF16)


def scatter_kernel(asked_ref, arrived_ref, out_ref):
    head, tail = spread(asked_ref[...])
    head_across = head.astype(F32).T
    tail_across = tail.astype(F32).T
    half = WIDTH // 2
    first = (iota((BLOCK, SENT), 1) & 7) < 4
    rows = (iota((BLOCK, SENT), 0) + 1).astype(F32)
    main = arrived_ref[:, :WIDTH]
    rest = arrived_ref[:, WIDTH:]
    for k in range(SHARD_ROWS // BLOCK):
        here = rows + float(BLOCK * k)
        hot_head = one_hot(head_across == here)
        in_tail = tail_across == here
        total = dot(hot_head, main)
        out = slice(k * BLOCK, (k + 1) * BLOCK)
        out_ref[out, :half] = (total[:, :half] + dot(one_hot(in_tail & first), rest)).astype(BF16)
        out_ref[out, half:] = (
            total[:, half:] + dot(one_hot(in_tail & jnp.logical_not(first)), rest)
        ).astype(BF16)


def sum_kernel(parts_ref, out_ref):
    total = parts_ref[0].astype(F32)
    for k in range(1, GROUPS):
        total += parts_ref[k].astype(F32)
    out_ref[...] = total


SCALAR = pl.BlockSpec(memory_space=pltpu.SMEM)
WHOLE = pl.BlockSpec(memory_space=pltpu.VMEM)


def run(kernel, name, outs, *args, scalars=0, scratch=()):
    single = not isinstance(outs, (list, tuple))
    return pl.pallas_call(
        kernel,
        out_shape=outs,
        in_specs=[SCALAR] * scalars + [WHOLE] * (len(args) - scalars),
        out_specs=WHOLE if single else [WHOLE] * len(outs),
        scratch_shapes=scratch,
        compiler_params=pltpu.CompilerParams(vmem_limit_bytes=40 * 1024 * 1024),
        name=name,
    )(*args)


def shape(*dims, dtype=BF16):
    return jax.ShapeDtypeStruct(dims, dtype)


def swap(array, axis, groups=None):
    return lax.all_to_all(
        array, axis, split_axis=0, concat_axis=0, tiled=True, axis_index_groups=groups
    )


def local(item_ids, history_len, item_slot, table_slab, proj_in, proj_out, upstream):
    upstream = upstream[0]
    requests, info = run(
        index_kernel,
        "index",
        [shape(SENT, BLOCK, dtype=jnp.int32), shape(8, BLOCK, dtype=jnp.int32)],
        history_len,
        item_ids,
        item_slot.reshape(BLOCK, BLOCK),
        scalars=1,
    )
    asked = swap(requests.reshape(TABLES, MAIN, BLOCK), "table").reshape(SENT, BLOCK)
    d_gated = run(
        cotangent_kernel,
        "cotangent",
        shape(BLOCK, WIDTH, dtype=F32),
        history_len,
        upstream,
        proj_out,
        scalars=1,
    )
    rows_out = run(gather_kernel, "gather", shape(SENT, PACKED), asked, table_slab)
    rows = swap(rows_out.reshape(TABLES, MAIN, PACKED), "table").reshape(SENT, PACKED)
    send, embedded, gate, slope = run(
        project_kernel,
        "project",
        [
            shape(GROUPS, PIECE, HEAD_DIM),
            shape(BLOCK, WIDTH),
            shape(BLOCK, WIDTH),
            shape(BLOCK, 2 * WIDTH, dtype=F32),
        ],
        info,
        rows,
        proj_in,
        d_gated,
    )
    recv = swap(send, "ctx")
    att, d_hat, stats = run(
        attend_kernel,
        "attend",
        [
            shape(HEAD_DIM, SPAN, dtype=F32),
            shape(HEAD_DIM, SPAN, dtype=F32),
            shape(HEADS, 8, SPAN, dtype=F32),
        ],
        recv,
    )
    lines = [[HEADS * g + h for h in range(HEADS)] for g in range(GROUPS // HEADS)]
    stats = swap(stats, "ctx", lines)
    send_back = run(
        backward_kernel,
        "backward",
        shape(GROUPS, PIECE, HEAD_DIM),
        recv,
        att,
        d_hat,
        stats,
        scratch=[pltpu.VMEM((HEAD_DIM, SPAN), F32)],
    )
    back = swap(send_back, "ctx")
    outgoing, att_hat = run(
        finish_kernel,
        "finish",
        [shape(SENT, PACKED), shape(BLOCK, WIDTH, dtype=F32)],
        history_len,
        info,
        back,
        embedded,
        slope,
        d_gated,
        upstream,
        proj_in,
        scalars=1,
    )
    arrived = swap(outgoing.reshape(TABLES, MAIN, PACKED), "table").reshape(SENT, PACKED)
    layer_out = run(
        output_kernel,
        "output",
        shape(BLOCK, WIDTH),
        history_len,
        att_hat,
        gate,
        embedded,
        proj_out,
        scalars=1,
    )
    sums = run(scatter_kernel, "scatter", shape(SHARD_ROWS, WIDTH), asked, arrived)
    parts = swap(sums.reshape(GROUPS, SHARD_ROWS // GROUPS, WIDTH), "ctx")
    table_grad = run(
        sum_kernel, "total", shape(SHARD_ROWS // GROUPS, WIDTH, dtype=F32), parts
    )
    return (layer_out[None], table_grad)


def solution(mesh):
    placed = (
        P("table", "ctx"),
        P("table"),
        P(),
        P("table", None),
        P(),
        P(),
        P("table", "ctx", None),
    )
    return jax.shard_map(
        local,
        mesh=mesh,
        in_specs=placed,
        out_specs=(P("table", "ctx", None), P(("table", "ctx"), None)),
        check_vma=False,
    )
```

```python
import jax
import jax.numpy as jnp
from jax import lax
from jax.experimental import pallas as pl
from jax.experimental.pallas import tpu as pltpu
from jax.sharding import PartitionSpec as P

EPSILON = 1e-05
BLOCK = 128
WIDTH = 512
HEADS = 4
HEAD_DIM = 128
TABLES = 32
GROUPS = 16
SHARD_ROWS = 512
QUERIES = BLOCK // HEADS
SEQ = BLOCK * GROUPS
SPAN = 4 * BLOCK
SCALE = HEAD_DIM ** (-0.5)
PIECE = 2 * BLOCK + 2 * QUERIES
MAIN = 8
SENT = TABLES * MAIN
PACKED = WIDTH + WIDTH // 2

F32 = jnp.float32
BF16 = jnp.bfloat16


def dot(a, b):
    return jnp.dot(a, b, preferred_element_type=F32)


def dot_nt(a, b):
    return lax.dot_general(a, b, (((1,), (1,)), ((), ())), preferred_element_type=F32)


def dot_tn(a, b):
    return lax.dot_general(a, b, (((0,), (0,)), ((), ())), preferred_element_type=F32)


def iota(shape, dim):
    return lax.broadcasted_iota(jnp.int32, shape, dim)


def one_hot(mask):
    return jnp.where(mask, 1.0, 0.0).astype(BF16)


def normalize(values):
    centre = values - jnp.mean(values, axis=-1, keepdims=True)
    scale_inv = lax.rsqrt(jnp.mean(centre * centre, axis=-1, keepdims=True) + EPSILON)
    return (centre * scale_inv, scale_inv)


def silu_and_slope(values):
    half = 0.5 * values
    th = jnp.tanh(half)
    out = half + half * th
    return out, 0.5 * ((1.0 + th) + out * (1.0 - th))


def norm_back(grad, normed, scale_inv):
    return scale_inv * (
        grad
        - jnp.mean(grad, axis=-1, keepdims=True)
        - normed * jnp.mean(grad * normed, axis=-1, keepdims=True)
    )


def index_kernel(length_ref, ids_ref, slot_ref, send_ref, info_ref):
    ids = ids_ref[...]
    event = iota((1, BLOCK), 1)
    length = length_ref[...]
    valid = lax.axis_index("ctx") * BLOCK + event < length
    row = iota((BLOCK, BLOCK), 0)
    table = slot_ref[...]
    rows_hot = one_hot(row == (ids >> 7))
    high = dot_tn((table >> 7).astype(F32).astype(BF16), rows_hot)
    low = dot_tn((table & 127).astype(F32).astype(BF16), rows_hot)
    both = jnp.where(row == (ids & 127), high * 128.0 + low, 0.0)
    slots = jnp.sum(both, axis=0, keepdims=True).astype(jnp.int32)
    owner = jnp.where(valid, slots >> 9, TABLES)
    wanted = (slots & (SHARD_ROWS - 1)) + 1
    owned = iota((TABLES, BLOCK), 0) == owner
    owned_hot = one_hot(owned)
    earlier = dot(owned_hot, one_hot(row < iota((BLOCK, BLOCK), 1)))
    rank = jnp.sum(jnp.where(owned, earlier, 0.0), axis=0, keepdims=True).astype(jnp.int32)
    head = jnp.where(valid & (rank < MAIN), owner * MAIN + rank, -1000)
    tail = jnp.where(valid & (rank >= MAIN), owner * MAIN + rank - MAIN, -1000)
    lengths = jnp.broadcast_to(length, (6, BLOCK))
    info_ref[...] = jnp.concatenate([head, tail, lengths], axis=0)
    ranked = jnp.where(row < BLOCK // 2, row & 7, MAIN + (row & 3)) == rank
    wanted_high = jnp.where(ranked, (wanted >> 5).astype(F32), 0.0).astype(BF16)
    wanted_low = jnp.where(ranked, (wanted & 31).astype(F32), 0.0).astype(BF16)
    asked = dot_nt(owned_hot, wanted_high) * 32.0 + dot_nt(owned_hot, wanted_low)
    send_ref[...] = asked.astype(jnp.int32)


def asked_rows(asked_ref):
    asked = asked_ref[...].reshape(TABLES, BLOCK).astype(F32)
    turned = pltpu.roll(asked, BLOCK // 2, 1)
    left = iota((TABLES, BLOCK), 1) < BLOCK // 2
    both = []
    for wanted in (jnp.where(left, asked, turned), jnp.where(left, turned, asked)):
        parts = []
        for k in range(SENT // BLOCK):
            own = iota((TABLES, BLOCK), 0) == (iota((TABLES, BLOCK), 1) >> 3) + k * BLOCK // MAIN
            parts.append(jnp.sum(jnp.where(own, wanted, 0.0), axis=0, keepdims=True))
        both.append(jnp.concatenate(parts, axis=1))
    return both


def gather_kernel(asked_ref, slab_ref, out_ref, rows_ref):
    head, tail = asked_rows(asked_ref)
    first = (iota((1, SENT), 1) & 7) < 4
    tail_first = jnp.where(first, tail, 0.0)
    tail_second = jnp.where(first, 0.0, tail)
    rows_ref[...] = jnp.concatenate(
        [head, tail_first, tail_second, head, tail_first, tail_second, head, tail], axis=0
    )
    half = WIDTH // 2
    row = (iota((SHARD_ROWS, SENT), 0) + 1).astype(F32)
    out_ref[:, :WIDTH] = dot_tn(one_hot(row == head), slab_ref[...]).astype(BF16)
    rest = dot_tn(one_hot(row == tail_first), slab_ref[:, :half])
    rest += dot_tn(one_hot(row == tail_second), slab_ref[:, half:])
    out_ref[:, WIDTH:] = rest.astype(BF16)


def valid_rows(d_gated_ref):
    length = d_gated_ref[BLOCK + 2 : BLOCK + 3, 0:1].astype(jnp.int32)
    return lax.axis_index("ctx") * BLOCK + iota((BLOCK, WIDTH), 0) < length


def place_masks(d_gated_ref):
    place = iota((SENT, BLOCK), 0)
    head = d_gated_ref[BLOCK : BLOCK + 1, :BLOCK].astype(jnp.int32)
    tail = d_gated_ref[BLOCK + 1 : BLOCK + 2, :BLOCK].astype(jnp.int32)
    return one_hot(place == head), one_hot(place == tail), one_hot(place == tail + 4)


def prepare_kernel(slab_ref, info_ref, upstream_ref, proj_out_ref, narrow_ref, d_gated_ref):
    narrow_ref[...] = slab_ref[...].astype(BF16)
    place = lax.axis_index("ctx") * BLOCK + iota((BLOCK, WIDTH), 0)
    d_out = jnp.where(place < info_ref[2:3, 0:1], upstream_ref[...], jnp.zeros((), BF16))
    d_gated_ref[:BLOCK, :] = dot_nt(d_out, proj_out_ref[...])
    d_gated_ref[BLOCK:, :BLOCK] = info_ref[...].astype(F32)
    d_gated_ref[BLOCK:, BLOCK:] = jnp.zeros((8, WIDTH - BLOCK), F32)


def project_kernel(
    rows_ref, proj_in_ref, d_gated_ref, send_ref, embedded_ref, gate_ref, slope_ref
):
    in_head, in_first, in_second = place_masks(d_gated_ref)
    half = WIDTH // 2
    rest = rows_ref[:, WIDTH:]
    embedded = dot_tn(in_head, rows_ref[:, :WIDTH]) + jnp.concatenate(
        [dot_tn(in_first, rest), dot_tn(in_second, rest)], axis=1
    )
    valid = valid_rows(d_gated_ref)
    embedded = jnp.where(valid, embedded, 0.0)
    embedded_ref[...] = embedded.astype(BF16)
    normed = normalize(embedded)[0].astype(BF16)

    def part(k):
        return dot(normed, proj_in_ref[:, k * WIDTH : (k + 1) * WIDTH])

    gate_part = part(0)
    value_part = part(1)
    gate, slope_ref[:, :WIDTH] = silu_and_slope(gate_part)
    value, slope_ref[:, WIDTH:] = silu_and_slope(value_part)
    gate, value = gate.astype(BF16), value.astype(BF16)
    gate_ref[...] = gate
    value = jnp.where(valid, value, jnp.zeros((), BF16))
    query = part(2).astype(BF16)
    key = jnp.where(valid, part(3), 0.0).astype(BF16)
    d_hat = (d_gated_ref[:BLOCK, :] * gate.astype(F32)).astype(BF16)
    for h in range(HEADS):
        cols = slice(h * HEAD_DIM, (h + 1) * HEAD_DIM)
        for g in range(HEADS):
            rows = slice(g * QUERIES, (g + 1) * QUERIES)
            chunk = HEADS * g + h
            send_ref[chunk, 0:BLOCK, :] = key[:, cols]
            send_ref[chunk, BLOCK : 2 * BLOCK, :] = value[:, cols]
            send_ref[chunk, 2 * BLOCK : 2 * BLOCK + QUERIES, :] = query[rows, cols]
            send_ref[chunk, 2 * BLOCK + QUERIES :, :] = d_hat[rows, cols]


def allowed_mask():
    group = lax.axis_index("ctx") // HEADS
    lane = iota((SPAN, BLOCK), 1)
    place = (lane // QUERIES) * BLOCK + group * QUERIES + lane % QUERIES
    return iota((SPAN, BLOCK), 0) <= place


def span_keys(recv_ref, j):
    chunks = slice(4 * j, 4 * j + 4)
    key = recv_ref[chunks, 0:BLOCK, :].reshape(SPAN, HEAD_DIM)
    value = recv_ref[chunks, BLOCK : 2 * BLOCK, :].reshape(SPAN, HEAD_DIM)
    return key, value


def attend_kernel(recv_ref, att_ref, d_hat_ref, stats_ref):
    query = recv_ref[:, 2 * BLOCK : 2 * BLOCK + QUERIES, :].reshape(SPAN, HEAD_DIM)
    mask = allowed_mask()
    for j in range(4):
        key, value = span_keys(recv_ref, j)
        start = j * BLOCK
        half = dot_nt(key, query[start:, :]) * (0.5 * SCALE)
        weight = half + half * jnp.tanh(half)
        weight = jnp.concatenate(
            [jnp.where(mask, weight[:, :BLOCK], 0.0), weight[:, BLOCK:]], axis=1
        ) if j < 3 else jnp.where(mask, weight, 0.0)
        part = dot_tn(value, weight.astype(BF16))
        if j == 0:
            att_ref[...] = part
        else:
            att_ref[:, start:] += part
    d_hat = recv_ref[:, 2 * BLOCK + QUERIES :, :].reshape(SPAN, HEAD_DIM)
    d_hat = d_hat.astype(F32).T
    d_hat_ref[...] = d_hat
    att = att_ref[...]
    mean = jnp.mean(att, axis=0, keepdims=True)
    centre = att - mean
    d_mean = jnp.mean(d_hat, axis=0, keepdims=True)
    spread_sum = jnp.sum(centre * centre, axis=0, keepdims=True)
    cross_sum = jnp.sum(centre * (d_hat - d_mean), axis=0, keepdims=True)
    rows = jnp.concatenate(
        [mean, spread_sum, d_mean, cross_sum, mean, spread_sum, d_mean, cross_sum], axis=0
    )
    for k in range(HEADS):
        stats_ref[k] = rows


def backward_kernel(recv_ref, att_ref, d_hat_ref, stats_ref, send_ref, d_query_ref):
    query = recv_ref[:, 2 * BLOCK : 2 * BLOCK + QUERIES, :].reshape(SPAN, HEAD_DIM)
    mask = allowed_mask()
    stats = [stats_ref[k] for k in range(HEADS)]

    def average(row):
        return sum(s[row : row + 1, :] for s in stats) / HEADS

    mean, d_mean = average(0), average(2)
    spread_mean = average(1) / HEAD_DIM + sum(
        (s[0:1, :] - mean) * (s[0:1, :] - mean) for s in stats
    ) / HEADS
    cross_mean = average(3) / HEAD_DIM + sum(
        (s[0:1, :] - mean) * (s[2:3, :] - d_mean) for s in stats
    ) / HEADS
    inv = lax.rsqrt(spread_mean + EPSILON)
    att = att_ref[...]
    att_hat = (att - mean) * inv
    d_att = (inv * (d_hat_ref[...] - d_mean - att_hat * (inv * cross_mean))).astype(BF16)
    out_att = att.T.astype(BF16)
    for j in range(4):
        key, value = span_keys(recv_ref, j)
        start = j * BLOCK
        half = dot_nt(key, query[start:, :]) * (0.5 * SCALE)
        th = jnp.tanh(half)
        weight = half + half * th
        slope = (0.5 * SCALE) * ((1.0 + th) + weight * (1.0 - th))
        d_score = dot(value, d_att[:, start:]) * slope

        def masked(values):
            first = jnp.where(mask, values[:, :BLOCK], 0.0)
            if j == 3:
                return first.astype(BF16)
            return jnp.concatenate([first, values[:, BLOCK:]], axis=1).astype(BF16)

        weight, d_score = masked(weight), masked(d_score)
        d_key = dot(d_score, query[start:, :]).astype(BF16)
        d_value = dot_nt(weight, d_att[:, start:]).astype(BF16)
        part = dot_tn(key, d_score)
        if j == 0:
            d_query_ref[...] = part
        else:
            d_query_ref[:, start:] += part
        for k in range(4):
            rows = slice(k * BLOCK, (k + 1) * BLOCK)
            send_ref[4 * j + k, 0:BLOCK, :] = d_key[rows]
            send_ref[4 * j + k, BLOCK : 2 * BLOCK, :] = d_value[rows]
    d_query = d_query_ref[...].T.astype(BF16)
    for c in range(GROUPS):
        rows = slice(c * QUERIES, (c + 1) * QUERIES)
        send_ref[c, 2 * BLOCK : 2 * BLOCK + QUERIES, :] = d_query[rows]
        send_ref[c, 2 * BLOCK + QUERIES :, :] = out_att[rows]


def collect(recv_ref, first, rows):
    return jnp.concatenate(
        [
            jnp.concatenate([recv_ref[HEADS * g + h, first : first + rows, :] for g in range(HEADS)], axis=0)
            for h in range(HEADS)
        ],
        axis=1,
    ).astype(F32)


def collect_sum(recv_ref, first):
    def head(h):
        return sum(
            recv_ref[HEADS * g + h, first : first + BLOCK, :].astype(F32) for g in range(HEADS)
        )

    return jnp.concatenate([head(h) for h in range(HEADS)], axis=1)


def finish_kernel(
    recv_ref,
    embedded_ref,
    gate_ref,
    slope_ref,
    d_gated_ref,
    upstream_ref,
    proj_in_ref,
    out_ref,
    gated_ref,
):
    att_hat = normalize(collect(recv_ref, 2 * BLOCK + QUERIES, QUERIES))[0]
    valid = valid_rows(d_gated_ref)
    gated_ref[...] = jnp.where(valid, att_hat * gate_ref[...].astype(F32), 0.0).astype(BF16)
    d_value = collect_sum(recv_ref, BLOCK) * slope_ref[:, WIDTH:]
    d_gate = d_gated_ref[:BLOCK, :] * att_hat * slope_ref[:, :WIDTH]
    d_query = collect(recv_ref, 2 * BLOCK, QUERIES)
    d_key = collect_sum(recv_ref, 0)
    d_normed = jnp.zeros((BLOCK, WIDTH), F32)
    for k, part in enumerate((d_gate, d_value, d_query, d_key)):
        d_normed += dot_nt(part.astype(BF16), proj_in_ref[:, k * WIDTH : (k + 1) * WIDTH])
    normed, inv_std = normalize(embedded_ref[...].astype(F32))
    d_embedded = upstream_ref[...].astype(F32) + norm_back(d_normed, normed, inv_std)
    d_embedded = jnp.where(valid, d_embedded, 0.0).astype(BF16)
    in_head, in_first, in_second = place_masks(d_gated_ref)
    half = WIDTH // 2
    out_ref[:, :WIDTH] = dot(in_head, d_embedded).astype(BF16)
    out_ref[:, WIDTH:] = (
        dot(in_first, d_embedded[:, :half]) + dot(in_second, d_embedded[:, half:])
    ).astype(BF16)


def scatter_kernel(wanted_ref, arrived_ref, out_ref):
    half = WIDTH // 2
    rest = arrived_ref[:, WIDTH:]
    row = (iota((SHARD_ROWS, SENT), 0) + 1).astype(F32)
    total = dot(one_hot(row == wanted_ref[0:1, :]), arrived_ref[:, :WIDTH])
    for k, start in enumerate((0, half)):
        tail = dot(one_hot(row == wanted_ref[k + 1 : k + 2, :]), rest)
        out_ref[:, start : start + half] = (total[:, start : start + half] + tail).astype(BF16)


def output_kernel(parts_ref, gated_ref, embedded_ref, proj_out_ref, grad_ref, out_ref):
    output = embedded_ref[...].astype(F32) + dot(gated_ref[...], proj_out_ref[...])
    out_ref[...] = output.astype(BF16)
    total = parts_ref[0].astype(F32)
    for k in range(1, GROUPS):
        total += parts_ref[k].astype(F32)
    grad_ref[...] = total


WHOLE = pl.BlockSpec(memory_space=pltpu.VMEM)


def run(kernel, name, outs, *args, scratch=(), vmem=40):
    single = not isinstance(outs, (list, tuple))
    return pl.pallas_call(
        kernel,
        out_shape=outs,
        in_specs=[WHOLE] * len(args),
        out_specs=WHOLE if single else [WHOLE] * len(outs),
        scratch_shapes=scratch,
        compiler_params=pltpu.CompilerParams(vmem_limit_bytes=vmem * 1024 * 1024),
        name=name,
    )(*args)


def shape(*dims, dtype=BF16):
    return jax.ShapeDtypeStruct(dims, dtype)


def swap(array, axis, groups=None):
    return lax.all_to_all(
        array, axis, split_axis=0, concat_axis=0, tiled=True, axis_index_groups=groups
    )


def local(item_ids, history_len, item_slot, table_slab, proj_in, proj_out, upstream):
    upstream = upstream[0]
    requests, info = run(
        index_kernel,
        "index",
        [shape(TABLES, BLOCK, dtype=jnp.int32), shape(8, BLOCK, dtype=jnp.int32)],
        history_len.reshape(1, 1),
        item_ids,
        item_slot.reshape(BLOCK, BLOCK),
        vmem=60,
    )
    asked = swap(requests.reshape(TABLES, 1, BLOCK), "table")
    slab, d_gated = run(
        prepare_kernel,
        "prepare",
        [shape(SHARD_ROWS, WIDTH), shape(BLOCK + 8, WIDTH, dtype=F32)],
        table_slab,
        info,
        upstream,
        proj_out,
    )
    rows_out, wanted = run(
        gather_kernel, "gather", [shape(SENT, PACKED), shape(8, SENT, dtype=F32)], asked, slab
    )
    rows = swap(rows_out.reshape(TABLES, MAIN, PACKED), "table").reshape(SENT, PACKED)
    send, embedded, gate, slope = run(
        project_kernel,
        "project",
        [
            shape(GROUPS, PIECE, HEAD_DIM),
            shape(BLOCK, WIDTH),
            shape(BLOCK, WIDTH),
            shape(BLOCK, 2 * WIDTH, dtype=F32),
        ],
        rows,
        proj_in,
        d_gated,
    )
    recv = swap(send, "ctx")
    att, d_hat, stats = run(
        attend_kernel,
        "attend",
        [
            shape(HEAD_DIM, SPAN, dtype=F32),
            shape(HEAD_DIM, SPAN, dtype=F32),
            shape(HEADS, 8, SPAN, dtype=F32),
        ],
        recv,
    )
    lines = [[HEADS * g + h for h in range(HEADS)] for g in range(GROUPS // HEADS)]
    stats = swap(stats, "ctx", lines)
    send_back = run(
        backward_kernel,
        "backward",
        shape(GROUPS, PIECE, HEAD_DIM),
        recv,
        att,
        d_hat,
        stats,
        scratch=[pltpu.VMEM((HEAD_DIM, SPAN), F32)],
    )
    back = swap(send_back, "ctx")
    outgoing, gated = run(
        finish_kernel,
        "finish",
        [shape(SENT, PACKED), shape(BLOCK, WIDTH)],
        back,
        embedded,
        gate,
        slope,
        d_gated,
        upstream,
        proj_in,
    )
    arrived = swap(outgoing.reshape(TABLES, MAIN, PACKED), "table").reshape(SENT, PACKED)
    sums = run(scatter_kernel, "scatter", shape(SHARD_ROWS, WIDTH), wanted, arrived)
    parts = swap(sums.reshape(GROUPS, SHARD_ROWS // GROUPS, WIDTH), "ctx")
    table_grad, layer_out = run(
        output_kernel,
        "output",
        [shape(SHARD_ROWS // GROUPS, WIDTH, dtype=F32), shape(BLOCK, WIDTH)],
        parts,
        gated,
        embedded,
        proj_out,
    )
    return (layer_out[None], table_grad)


def solution(mesh):
    placed = (
        P("table", "ctx"),
        P("table"),
        P(),
        P("table", None),
        P(),
        P(),
        P("table", "ctx", None),
    )
    return jax.shard_map(
        local,
        mesh=mesh,
        in_specs=placed,
        out_specs=(P("table", "ctx", None), P(("table", "ctx"), None)),
        check_vma=False,
    )
```

```python
import jax
import jax.numpy as jnp
from jax import lax
from jax.experimental import pallas as pl
from jax.experimental.pallas import tpu as pltpu
from jax.sharding import PartitionSpec as P

EPSILON = 1e-05
BLOCK = 128
WIDTH = 512
HEADS = 4
HEAD_DIM = 128
TABLES = 32
GROUPS = 16
SHARD_ROWS = 512
QUERIES = BLOCK // HEADS
SEQ = BLOCK * GROUPS
SPAN = 4 * BLOCK
SCALE = HEAD_DIM ** (-0.5)
PIECE = 2 * BLOCK + 2 * QUERIES
MAIN = 8
SENT = TABLES * MAIN
PACKED = WIDTH + WIDTH // 2

F32 = jnp.float32
BF16 = jnp.bfloat16


def dot(a, b):
    return jnp.dot(a, b, preferred_element_type=F32)


def dot_nt(a, b):
    return lax.dot_general(a, b, (((1,), (1,)), ((), ())), preferred_element_type=F32)


def dot_tn(a, b):
    return lax.dot_general(a, b, (((0,), (0,)), ((), ())), preferred_element_type=F32)


def iota(shape, dim):
    return lax.broadcasted_iota(jnp.int32, shape, dim)


def one_hot(mask):
    return jnp.where(mask, 1.0, 0.0).astype(BF16)


def normalize(values):
    centre = values - jnp.mean(values, axis=-1, keepdims=True)
    scale_inv = lax.rsqrt(jnp.mean(centre * centre, axis=-1, keepdims=True) + EPSILON)
    return (centre * scale_inv, scale_inv)


def silu_and_slope(values):
    half = 0.5 * values
    th = jnp.tanh(half)
    out = half + half * th
    return out, 0.5 * ((1.0 + th) + out * (1.0 - th))


def norm_back(grad, normed, scale_inv):
    return scale_inv * (
        grad
        - jnp.mean(grad, axis=-1, keepdims=True)
        - normed * jnp.mean(grad * normed, axis=-1, keepdims=True)
    )


def index_kernel(length_ref, ids_ref, slot_ref, send_ref, info_ref):
    ids = ids_ref[...]
    event = iota((1, BLOCK), 1)
    length = length_ref[...]
    valid = lax.axis_index("ctx") * BLOCK + event < length
    row = iota((BLOCK, BLOCK), 0)
    table = slot_ref[...]
    rows_hot = one_hot(row == (ids >> 7))
    high = dot_tn((table >> 7).astype(F32).astype(BF16), rows_hot)
    low = dot_tn((table & 127).astype(F32).astype(BF16), rows_hot)
    both = jnp.where(row == (ids & 127), high * 128.0 + low, 0.0)
    slots = jnp.sum(both, axis=0, keepdims=True).astype(jnp.int32)
    shard = slots >> 9
    owner = jnp.where(valid, 2 * ((11 * (shard >> 1)) & 15) + (shard & 1), TABLES)
    wanted = (slots & (SHARD_ROWS - 1)) + 1
    owned = iota((TABLES, BLOCK), 0) == owner
    owned_hot = one_hot(owned)
    earlier = dot(owned_hot, one_hot(row < iota((BLOCK, BLOCK), 1)))
    rank = jnp.sum(jnp.where(owned, earlier, 0.0), axis=0, keepdims=True).astype(jnp.int32)
    head = jnp.where(valid & (rank < MAIN), owner * MAIN + rank, -1000)
    tail = jnp.where(valid & (rank >= MAIN), owner * MAIN + rank - MAIN, -1000)
    lengths = jnp.broadcast_to(length, (6, BLOCK))
    info_ref[...] = jnp.concatenate([head, tail, lengths], axis=0)
    ranked = jnp.where(row < BLOCK // 2, row & 7, MAIN + (row & 3)) == rank
    wanted_high = jnp.where(ranked, (wanted >> 5).astype(F32), 0.0).astype(BF16)
    wanted_low = jnp.where(ranked, (wanted & 31).astype(F32), 0.0).astype(BF16)
    asked = dot_nt(owned_hot, wanted_high) * 32.0 + dot_nt(owned_hot, wanted_low)
    send_ref[...] = asked.astype(jnp.int32)


def asked_rows(asked_ref):
    asked = asked_ref[...].reshape(TABLES, BLOCK).astype(F32)
    turned = pltpu.roll(asked, BLOCK // 2, 1)
    left = iota((TABLES, BLOCK), 1) < BLOCK // 2
    both = []
    for wanted in (jnp.where(left, asked, turned), jnp.where(left, turned, asked)):
        parts = []
        for k in range(SENT // BLOCK):
            own = iota((TABLES, BLOCK), 0) == (iota((TABLES, BLOCK), 1) >> 3) + k * BLOCK // MAIN
            parts.append(jnp.sum(jnp.where(own, wanted, 0.0), axis=0, keepdims=True))
        both.append(jnp.concatenate(parts, axis=1))
    return both


def gather_kernel(asked_ref, slab_ref, out_ref, rows_ref):
    head, tail = asked_rows(asked_ref)
    first = (iota((1, SENT), 1) & 7) < 4
    tail_first = jnp.where(first, tail, 0.0)
    tail_second = jnp.where(first, 0.0, tail)
    rows_ref[...] = jnp.concatenate(
        [head, tail_first, tail_second, head, tail_first, tail_second, head, tail], axis=0
    )
    half = WIDTH // 2
    row = (iota((SHARD_ROWS, SENT), 0) + 1).astype(F32)
    out_ref[:, :WIDTH] = dot_tn(one_hot(row == head), slab_ref[...]).astype(BF16)
    rest = dot_tn(one_hot(row == tail_first), slab_ref[:, :half])
    rest += dot_tn(one_hot(row == tail_second), slab_ref[:, half:])
    out_ref[:, WIDTH:] = rest.astype(BF16)


def valid_rows(d_gated_ref):
    length = d_gated_ref[BLOCK + 2 : BLOCK + 3, 0:1].astype(jnp.int32)
    return lax.axis_index("ctx") * BLOCK + iota((BLOCK, WIDTH), 0) < length


def place_masks(d_gated_ref):
    place = iota((SENT, BLOCK), 0)
    head = d_gated_ref[BLOCK : BLOCK + 1, :BLOCK].astype(jnp.int32)
    tail = d_gated_ref[BLOCK + 1 : BLOCK + 2, :BLOCK].astype(jnp.int32)
    return one_hot(place == head), one_hot(place == tail), one_hot(place == tail + 4)


def prepare_kernel(slab_ref, info_ref, upstream_ref, proj_out_ref, narrow_ref, d_gated_ref):
    narrow_ref[...] = slab_ref[...].astype(BF16)
    place = lax.axis_index("ctx") * BLOCK + iota((BLOCK, WIDTH), 0)
    d_out = jnp.where(place < info_ref[2:3, 0:1], upstream_ref[...], jnp.zeros((), BF16))
    d_gated_ref[:BLOCK, :] = dot_nt(d_out, proj_out_ref[...])
    d_gated_ref[BLOCK:, :BLOCK] = info_ref[...].astype(F32)
    d_gated_ref[BLOCK:, BLOCK:] = jnp.zeros((8, WIDTH - BLOCK), F32)


def project_kernel(
    rows_ref, proj_in_ref, d_gated_ref, send_ref, embedded_ref, gate_ref, slope_ref
):
    in_head, in_first, in_second = place_masks(d_gated_ref)
    half = WIDTH // 2
    rest = rows_ref[:, WIDTH:]
    embedded = dot_tn(in_head, rows_ref[:, :WIDTH]) + jnp.concatenate(
        [dot_tn(in_first, rest), dot_tn(in_second, rest)], axis=1
    )
    valid = valid_rows(d_gated_ref)
    embedded = jnp.where(valid, embedded, 0.0)
    embedded_ref[...] = embedded.astype(BF16)
    normed = normalize(embedded)[0].astype(BF16)

    def part(k):
        return dot(normed, proj_in_ref[:, k * WIDTH : (k + 1) * WIDTH])

    gate_part = part(0)
    value_part = part(1)
    gate, slope_ref[:, :WIDTH] = silu_and_slope(gate_part)
    value, slope_ref[:, WIDTH:] = silu_and_slope(value_part)
    gate, value = gate.astype(BF16), value.astype(BF16)
    gate_ref[...] = gate
    value = jnp.where(valid, value, jnp.zeros((), BF16))
    query = part(2).astype(BF16)
    key = jnp.where(valid, part(3), 0.0).astype(BF16)
    d_hat = (d_gated_ref[:BLOCK, :] * gate.astype(F32)).astype(BF16)
    for h in range(HEADS):
        cols = slice(h * HEAD_DIM, (h + 1) * HEAD_DIM)
        for g in range(HEADS):
            rows = slice(g * QUERIES, (g + 1) * QUERIES)
            chunk = HEADS * g + h
            send_ref[chunk, 0:BLOCK, :] = key[:, cols]
            send_ref[chunk, BLOCK : 2 * BLOCK, :] = value[:, cols]
            send_ref[chunk, 2 * BLOCK : 2 * BLOCK + QUERIES, :] = query[rows, cols]
            send_ref[chunk, 2 * BLOCK + QUERIES :, :] = d_hat[rows, cols]


def allowed_mask():
    group = lax.axis_index("ctx") // HEADS
    lane = iota((SPAN, BLOCK), 1)
    place = (lane // QUERIES) * BLOCK + group * QUERIES + lane % QUERIES
    return iota((SPAN, BLOCK), 0) <= place


def span_keys(recv_ref, j):
    chunks = slice(4 * j, 4 * j + 4)
    key = recv_ref[chunks, 0:BLOCK, :].reshape(SPAN, HEAD_DIM)
    value = recv_ref[chunks, BLOCK : 2 * BLOCK, :].reshape(SPAN, HEAD_DIM)
    return key, value


def attend_kernel(recv_ref, att_ref, d_hat_ref, stats_ref):
    query = recv_ref[:, 2 * BLOCK : 2 * BLOCK + QUERIES, :].reshape(SPAN, HEAD_DIM)
    mask = allowed_mask()
    for j in range(4):
        key, value = span_keys(recv_ref, j)
        start = j * BLOCK
        half = dot_nt(key, query[start:, :]) * (0.5 * SCALE)
        weight = half + half * jnp.tanh(half)
        weight = jnp.concatenate(
            [jnp.where(mask, weight[:, :BLOCK], 0.0), weight[:, BLOCK:]], axis=1
        ) if j < 3 else jnp.where(mask, weight, 0.0)
        part = dot_tn(value, weight.astype(BF16))
        if j == 0:
            att_ref[...] = part
        else:
            att_ref[:, start:] += part
    d_hat = recv_ref[:, 2 * BLOCK + QUERIES :, :].reshape(SPAN, HEAD_DIM)
    d_hat = d_hat.astype(F32).T
    d_hat_ref[...] = d_hat
    att = att_ref[...]
    mean = jnp.mean(att, axis=0, keepdims=True)
    centre = att - mean
    d_mean = jnp.mean(d_hat, axis=0, keepdims=True)
    spread_sum = jnp.sum(centre * centre, axis=0, keepdims=True)
    cross_sum = jnp.sum(centre * (d_hat - d_mean), axis=0, keepdims=True)
    rows = jnp.concatenate(
        [mean, spread_sum, d_mean, cross_sum, mean, spread_sum, d_mean, cross_sum], axis=0
    )
    for k in range(HEADS):
        stats_ref[k] = rows


def backward_kernel(recv_ref, att_ref, d_hat_ref, stats_ref, send_ref, d_query_ref):
    query = recv_ref[:, 2 * BLOCK : 2 * BLOCK + QUERIES, :].reshape(SPAN, HEAD_DIM)
    mask = allowed_mask()
    stats = [stats_ref[k] for k in range(HEADS)]

    def average(row):
        return sum(s[row : row + 1, :] for s in stats) / HEADS

    mean, d_mean = average(0), average(2)
    spread_mean = average(1) / HEAD_DIM + sum(
        (s[0:1, :] - mean) * (s[0:1, :] - mean) for s in stats
    ) / HEADS
    cross_mean = average(3) / HEAD_DIM + sum(
        (s[0:1, :] - mean) * (s[2:3, :] - d_mean) for s in stats
    ) / HEADS
    inv = lax.rsqrt(spread_mean + EPSILON)
    att = att_ref[...]
    att_hat = (att - mean) * inv
    d_att = (inv * (d_hat_ref[...] - d_mean - att_hat * (inv * cross_mean))).astype(BF16)
    out_att = att.T.astype(BF16)
    for j in range(4):
        key, value = span_keys(recv_ref, j)
        start = j * BLOCK
        half = dot_nt(key, query[start:, :]) * (0.5 * SCALE)
        th = jnp.tanh(half)
        weight = half + half * th
        slope = (0.5 * SCALE) * ((1.0 + th) + weight * (1.0 - th))
        d_score = dot(value, d_att[:, start:]) * slope

        def masked(values):
            first = jnp.where(mask, values[:, :BLOCK], 0.0)
            if j == 3:
                return first.astype(BF16)
            return jnp.concatenate([first, values[:, BLOCK:]], axis=1).astype(BF16)

        weight, d_score = masked(weight), masked(d_score)
        d_key = dot(d_score, query[start:, :]).astype(BF16)
        d_value = dot_nt(weight, d_att[:, start:]).astype(BF16)
        part = dot_tn(key, d_score)
        if j == 0:
            d_query_ref[...] = part
        else:
            d_query_ref[:, start:] += part
        for k in range(4):
            rows = slice(k * BLOCK, (k + 1) * BLOCK)
            send_ref[4 * j + k, 0:BLOCK, :] = d_key[rows]
            send_ref[4 * j + k, BLOCK : 2 * BLOCK, :] = d_value[rows]
    d_query = d_query_ref[...].T.astype(BF16)
    for c in range(GROUPS):
        rows = slice(c * QUERIES, (c + 1) * QUERIES)
        send_ref[c, 2 * BLOCK : 2 * BLOCK + QUERIES, :] = d_query[rows]
        send_ref[c, 2 * BLOCK + QUERIES :, :] = out_att[rows]


def collect(recv_ref, first, rows):
    return jnp.concatenate(
        [
            jnp.concatenate([recv_ref[HEADS * g + h, first : first + rows, :] for g in range(HEADS)], axis=0)
            for h in range(HEADS)
        ],
        axis=1,
    ).astype(F32)


def collect_sum(recv_ref, first):
    def head(h):
        return sum(
            recv_ref[HEADS * g + h, first : first + BLOCK, :].astype(F32) for g in range(HEADS)
        )

    return jnp.concatenate([head(h) for h in range(HEADS)], axis=1)


def finish_kernel(
    recv_ref,
    embedded_ref,
    gate_ref,
    slope_ref,
    d_gated_ref,
    upstream_ref,
    proj_in_ref,
    out_ref,
    gated_ref,
):
    att_hat = normalize(collect(recv_ref, 2 * BLOCK + QUERIES, QUERIES))[0]
    valid = valid_rows(d_gated_ref)
    gated_ref[...] = jnp.where(valid, att_hat * gate_ref[...].astype(F32), 0.0).astype(BF16)
    d_value = collect_sum(recv_ref, BLOCK) * slope_ref[:, WIDTH:]
    d_gate = d_gated_ref[:BLOCK, :] * att_hat * slope_ref[:, :WIDTH]
    d_query = collect(recv_ref, 2 * BLOCK, QUERIES)
    d_key = collect_sum(recv_ref, 0)
    d_normed = jnp.zeros((BLOCK, WIDTH), F32)
    for k, part in enumerate((d_gate, d_value, d_query, d_key)):
        d_normed += dot_nt(part.astype(BF16), proj_in_ref[:, k * WIDTH : (k + 1) * WIDTH])
    normed, inv_std = normalize(embedded_ref[...].astype(F32))
    d_embedded = upstream_ref[...].astype(F32) + norm_back(d_normed, normed, inv_std)
    d_embedded = jnp.where(valid, d_embedded, 0.0).astype(BF16)
    in_head, in_first, in_second = place_masks(d_gated_ref)
    half = WIDTH // 2
    out_ref[:, :WIDTH] = dot(in_head, d_embedded).astype(BF16)
    out_ref[:, WIDTH:] = (
        dot(in_first, d_embedded[:, :half]) + dot(in_second, d_embedded[:, half:])
    ).astype(BF16)


def scatter_kernel(wanted_ref, arrived_ref, out_ref):
    half = WIDTH // 2
    rest = arrived_ref[:, WIDTH:]
    row = (iota((SHARD_ROWS, SENT), 0) + 1).astype(F32)
    total = dot(one_hot(row == wanted_ref[0:1, :]), arrived_ref[:, :WIDTH])
    for k, start in enumerate((0, half)):
        tail = dot(one_hot(row == wanted_ref[k + 1 : k + 2, :]), rest)
        out_ref[:, start : start + half] = (total[:, start : start + half] + tail).astype(BF16)


def output_kernel(parts_ref, gated_ref, embedded_ref, proj_out_ref, grad_ref, out_ref):
    output = embedded_ref[...].astype(F32) + dot(gated_ref[...], proj_out_ref[...])
    out_ref[...] = output.astype(BF16)
    total = parts_ref[0].astype(F32)
    for k in range(1, GROUPS):
        total += parts_ref[k].astype(F32)
    grad_ref[...] = total


WHOLE = pl.BlockSpec(memory_space=pltpu.VMEM)


def run(kernel, name, outs, *args, scratch=(), vmem=40):
    single = not isinstance(outs, (list, tuple))
    return pl.pallas_call(
        kernel,
        out_shape=outs,
        in_specs=[WHOLE] * len(args),
        out_specs=WHOLE if single else [WHOLE] * len(outs),
        scratch_shapes=scratch,
        compiler_params=pltpu.CompilerParams(vmem_limit_bytes=vmem * 1024 * 1024),
        name=name,
    )(*args)


def shape(*dims, dtype=BF16):
    return jax.ShapeDtypeStruct(dims, dtype)


def swap(array, axis, groups=None):
    return lax.all_to_all(
        array, axis, split_axis=0, concat_axis=0, tiled=True, axis_index_groups=groups
    )


def local(item_ids, history_len, item_slot, table_slab, proj_in, proj_out, upstream):
    upstream = upstream[0]
    order = [[2 * ((3 * (p // 2)) % 16) + p % 2 for p in range(TABLES)]]
    requests, info = run(
        index_kernel,
        "index",
        [shape(TABLES, BLOCK, dtype=jnp.int32), shape(8, BLOCK, dtype=jnp.int32)],
        history_len.reshape(1, 1),
        item_ids,
        item_slot.reshape(BLOCK, BLOCK),
        vmem=60,
    )
    asked = swap(requests.reshape(TABLES, 1, BLOCK), "table", order)
    slab, d_gated = run(
        prepare_kernel,
        "prepare",
        [shape(SHARD_ROWS, WIDTH), shape(BLOCK + 8, WIDTH, dtype=F32)],
        table_slab,
        info,
        upstream,
        proj_out,
    )
    rows_out, wanted = run(
        gather_kernel, "gather", [shape(SENT, PACKED), shape(8, SENT, dtype=F32)], asked, slab
    )
    rows = swap(rows_out.reshape(TABLES, MAIN, PACKED), "table", order).reshape(SENT, PACKED)
    send, embedded, gate, slope = run(
        project_kernel,
        "project",
        [
            shape(GROUPS, PIECE, HEAD_DIM),
            shape(BLOCK, WIDTH),
            shape(BLOCK, WIDTH),
            shape(BLOCK, 2 * WIDTH, dtype=F32),
        ],
        rows,
        proj_in,
        d_gated,
    )
    recv = swap(send, "ctx")
    att, d_hat, stats = run(
        attend_kernel,
        "attend",
        [
            shape(HEAD_DIM, SPAN, dtype=F32),
            shape(HEAD_DIM, SPAN, dtype=F32),
            shape(HEADS, 8, SPAN, dtype=F32),
        ],
        recv,
    )
    lines = [[HEADS * g + h for h in range(HEADS)] for g in range(GROUPS // HEADS)]
    stats = swap(stats, "ctx", lines)
    send_back = run(
        backward_kernel,
        "backward",
        shape(GROUPS, PIECE, HEAD_DIM),
        recv,
        att,
        d_hat,
        stats,
        scratch=[pltpu.VMEM((HEAD_DIM, SPAN), F32)],
    )
    back = swap(send_back, "ctx")
    outgoing, gated = run(
        finish_kernel,
        "finish",
        [shape(SENT, PACKED), shape(BLOCK, WIDTH)],
        back,
        embedded,
        gate,
        slope,
        d_gated,
        upstream,
        proj_in,
    )
    arrived = swap(outgoing.reshape(TABLES, MAIN, PACKED), "table", order).reshape(SENT, PACKED)
    sums = run(scatter_kernel, "scatter", shape(SHARD_ROWS, WIDTH), wanted, arrived)
    parts = swap(sums.reshape(GROUPS, SHARD_ROWS // GROUPS, WIDTH), "ctx")
    table_grad, layer_out = run(
        output_kernel,
        "output",
        [shape(SHARD_ROWS // GROUPS, WIDTH, dtype=F32), shape(BLOCK, WIDTH)],
        parts,
        gated,
        embedded,
        proj_out,
    )
    return (layer_out[None], table_grad)


def solution(mesh):
    placed = (
        P("table", "ctx"),
        P("table"),
        P(),
        P("table", None),
        P(),
        P(),
        P("table", "ctx", None),
    )
    return jax.shard_map(
        local,
        mesh=mesh,
        in_specs=placed,
        out_specs=(P("table", "ctx", None), P(("table", "ctx"), None)),
        check_vma=False,
    )
```

```python
import jax
import jax.numpy as jnp
from jax import lax
from jax.experimental import pallas as pl
from jax.experimental.pallas import tpu as pltpu
from jax.sharding import PartitionSpec as P

EPSILON = 1e-05
BLOCK = 128
WIDTH = 512
HEADS = 4
HEAD_DIM = 128
TABLES = 32
GROUPS = 16
SHARD_ROWS = 512
QUERIES = BLOCK // HEADS
SEQ = BLOCK * GROUPS
SPAN = 4 * BLOCK
SCALE = HEAD_DIM ** (-0.5)
PIECE = 2 * BLOCK + 2 * QUERIES
MAIN = 8
SENT = TABLES * MAIN
PACKED = WIDTH + WIDTH // 2
ORDER = [0, 1, 2, 3, 7, 6, 5, 4, 8, 9, 10, 11, 15, 14, 13, 12]
PLACE = [ORDER.index(c) for c in range(GROUPS)]

F32 = jnp.float32
BF16 = jnp.bfloat16


def dot(a, b):
    return jnp.dot(a, b, preferred_element_type=F32)


def dot_nt(a, b):
    return lax.dot_general(a, b, (((1,), (1,)), ((), ())), preferred_element_type=F32)


def dot_tn(a, b):
    return lax.dot_general(a, b, (((0,), (0,)), ((), ())), preferred_element_type=F32)


def iota(shape, dim):
    return lax.broadcasted_iota(jnp.int32, shape, dim)


def one_hot(mask):
    return jnp.where(mask, 1.0, 0.0).astype(BF16)


def normalize(values):
    centre = values - jnp.mean(values, axis=-1, keepdims=True)
    scale_inv = lax.rsqrt(jnp.mean(centre * centre, axis=-1, keepdims=True) + EPSILON)
    return (centre * scale_inv, scale_inv)


def silu_and_slope(values):
    half = 0.5 * values
    th = jnp.tanh(half)
    out = half + half * th
    return out, 0.5 * ((1.0 + th) + out * (1.0 - th))


def norm_back(grad, normed, scale_inv):
    return scale_inv * (
        grad
        - jnp.mean(grad, axis=-1, keepdims=True)
        - normed * jnp.mean(grad * normed, axis=-1, keepdims=True)
    )


def index_kernel(length_ref, ids_ref, slot_ref, send_ref, info_ref):
    ids = ids_ref[...]
    event = iota((1, BLOCK), 1)
    length = length_ref[...]
    valid = lax.axis_index("ctx") * BLOCK + event < length
    row = iota((BLOCK, BLOCK), 0)
    table = slot_ref[...]
    rows_hot = one_hot(row == (ids >> 7))
    high = dot_tn((table >> 7).astype(F32).astype(BF16), rows_hot)
    low = dot_tn((table & 127).astype(F32).astype(BF16), rows_hot)
    both = jnp.where(row == (ids & 127), high * 128.0 + low, 0.0)
    slots = jnp.sum(both, axis=0, keepdims=True).astype(jnp.int32)
    shard = slots >> 9
    owner = jnp.where(valid, 2 * ((11 * (shard >> 1)) & 15) + (shard & 1), TABLES)
    wanted = (slots & (SHARD_ROWS - 1)) + 1
    owned = iota((TABLES, BLOCK), 0) == owner
    owned_hot = one_hot(owned)
    earlier = dot(owned_hot, one_hot(row < iota((BLOCK, BLOCK), 1)))
    rank = jnp.sum(jnp.where(owned, earlier, 0.0), axis=0, keepdims=True).astype(jnp.int32)
    head = jnp.where(valid & (rank < MAIN), owner * MAIN + rank, -1000)
    tail = jnp.where(valid & (rank >= MAIN), owner * MAIN + rank - MAIN, -1000)
    lengths = jnp.broadcast_to(length, (6, BLOCK))
    info_ref[...] = jnp.concatenate([head, tail, lengths], axis=0)
    ranked = jnp.where(row < BLOCK // 2, row & 7, MAIN + (row & 3)) == rank
    wanted_high = jnp.where(ranked, (wanted >> 5).astype(F32), 0.0).astype(BF16)
    wanted_low = jnp.where(ranked, (wanted & 31).astype(F32), 0.0).astype(BF16)
    asked = dot_nt(owned_hot, wanted_high) * 32.0 + dot_nt(owned_hot, wanted_low)
    send_ref[...] = asked.astype(jnp.int32)


def asked_rows(asked_ref):
    asked = asked_ref[...].reshape(TABLES, BLOCK).astype(F32)
    turned = pltpu.roll(asked, BLOCK // 2, 1)
    left = iota((TABLES, BLOCK), 1) < BLOCK // 2
    both = []
    for wanted in (jnp.where(left, asked, turned), jnp.where(left, turned, asked)):
        parts = []
        for k in range(SENT // BLOCK):
            own = iota((TABLES, BLOCK), 0) == (iota((TABLES, BLOCK), 1) >> 3) + k * BLOCK // MAIN
            parts.append(jnp.sum(jnp.where(own, wanted, 0.0), axis=0, keepdims=True))
        both.append(jnp.concatenate(parts, axis=1))
    return both


def gather_kernel(asked_ref, slab_ref, out_ref, rows_ref):
    head, tail = asked_rows(asked_ref)
    first = (iota((1, SENT), 1) & 7) < 4
    tail_first = jnp.where(first, tail, 0.0)
    tail_second = jnp.where(first, 0.0, tail)
    rows_ref[...] = jnp.concatenate(
        [head, tail_first, tail_second, head, tail_first, tail_second, head, tail], axis=0
    )
    half = WIDTH // 2
    row = (iota((SHARD_ROWS, SENT), 0) + 1).astype(F32)
    out_ref[:, :WIDTH] = dot_tn(one_hot(row == head), slab_ref[...]).astype(BF16)
    rest = dot_tn(one_hot(row == tail_first), slab_ref[:, :half])
    rest += dot_tn(one_hot(row == tail_second), slab_ref[:, half:])
    out_ref[:, WIDTH:] = rest.astype(BF16)


def valid_rows(d_gated_ref):
    length = d_gated_ref[BLOCK + 2 : BLOCK + 3, 0:1].astype(jnp.int32)
    return lax.axis_index("ctx") * BLOCK + iota((BLOCK, WIDTH), 0) < length


def place_masks(d_gated_ref):
    place = iota((SENT, BLOCK), 0)
    head = d_gated_ref[BLOCK : BLOCK + 1, :BLOCK].astype(jnp.int32)
    tail = d_gated_ref[BLOCK + 1 : BLOCK + 2, :BLOCK].astype(jnp.int32)
    return one_hot(place == head), one_hot(place == tail), one_hot(place == tail + 4)


def prepare_kernel(slab_ref, info_ref, upstream_ref, proj_out_ref, narrow_ref, d_gated_ref):
    narrow_ref[...] = slab_ref[...].astype(BF16)
    place = lax.axis_index("ctx") * BLOCK + iota((BLOCK, WIDTH), 0)
    d_out = jnp.where(place < info_ref[2:3, 0:1], upstream_ref[...], jnp.zeros((), BF16))
    d_gated_ref[:BLOCK, :] = dot_nt(d_out, proj_out_ref[...])
    d_gated_ref[BLOCK:, :BLOCK] = info_ref[...].astype(F32)
    d_gated_ref[BLOCK:, BLOCK:] = jnp.zeros((8, WIDTH - BLOCK), F32)


def project_kernel(
    rows_ref, proj_in_ref, d_gated_ref, send_ref, embedded_ref, gate_ref, slope_ref
):
    in_head, in_first, in_second = place_masks(d_gated_ref)
    half = WIDTH // 2
    rest = rows_ref[:, WIDTH:]
    embedded = dot_tn(in_head, rows_ref[:, :WIDTH]) + jnp.concatenate(
        [dot_tn(in_first, rest), dot_tn(in_second, rest)], axis=1
    )
    valid = valid_rows(d_gated_ref)
    embedded = jnp.where(valid, embedded, 0.0)
    embedded_ref[...] = embedded.astype(BF16)
    normed = normalize(embedded)[0].astype(BF16)

    def part(k):
        return dot(normed, proj_in_ref[:, k * WIDTH : (k + 1) * WIDTH])

    gate_part = part(0)
    value_part = part(1)
    gate, slope_ref[:, :WIDTH] = silu_and_slope(gate_part)
    value, slope_ref[:, WIDTH:] = silu_and_slope(value_part)
    gate, value = gate.astype(BF16), value.astype(BF16)
    gate_ref[...] = gate
    value = jnp.where(valid, value, jnp.zeros((), BF16))
    query = part(2).astype(BF16)
    key = jnp.where(valid, part(3), 0.0).astype(BF16)
    d_hat = (d_gated_ref[:BLOCK, :] * gate.astype(F32)).astype(BF16)
    for h in range(HEADS):
        cols = slice(h * HEAD_DIM, (h + 1) * HEAD_DIM)
        for g in range(HEADS):
            rows = slice(g * QUERIES, (g + 1) * QUERIES)
            chunk = PLACE[HEADS * g + h]
            send_ref[chunk, 0:BLOCK, :] = key[:, cols]
            send_ref[chunk, BLOCK : 2 * BLOCK, :] = value[:, cols]
            send_ref[chunk, 2 * BLOCK : 2 * BLOCK + QUERIES, :] = query[rows, cols]
            send_ref[chunk, 2 * BLOCK + QUERIES :, :] = d_hat[rows, cols]


def allowed_mask():
    group = lax.axis_index("ctx") // HEADS
    lane = iota((SPAN, BLOCK), 1)
    place = (lane // QUERIES) * BLOCK + group * QUERIES + lane % QUERIES
    return iota((SPAN, BLOCK), 0) <= place


def take(recv_ref, blocks, first, rows):
    return jnp.concatenate([recv_ref[PLACE[c], first : first + rows, :] for c in blocks], axis=0)


def span_keys(recv_ref, j):
    blocks = range(4 * j, 4 * j + 4)
    return take(recv_ref, blocks, 0, BLOCK), take(recv_ref, blocks, BLOCK, BLOCK)


def attend_kernel(recv_ref, att_ref, d_hat_ref, stats_ref):
    query = take(recv_ref, range(GROUPS), 2 * BLOCK, QUERIES)
    mask = allowed_mask()
    for j in range(4):
        key, value = span_keys(recv_ref, j)
        start = j * BLOCK
        half = dot_nt(key, query[start:, :]) * (0.5 * SCALE)
        weight = half + half * jnp.tanh(half)
        weight = jnp.concatenate(
            [jnp.where(mask, weight[:, :BLOCK], 0.0), weight[:, BLOCK:]], axis=1
        ) if j < 3 else jnp.where(mask, weight, 0.0)
        part = dot_tn(value, weight.astype(BF16))
        if j == 0:
            att_ref[...] = part
        else:
            att_ref[:, start:] += part
    d_hat = take(recv_ref, range(GROUPS), 2 * BLOCK + QUERIES, QUERIES)
    d_hat = d_hat.astype(F32).T
    d_hat_ref[...] = d_hat
    att = att_ref[...]
    mean = jnp.mean(att, axis=0, keepdims=True)
    centre = att - mean
    d_mean = jnp.mean(d_hat, axis=0, keepdims=True)
    spread_sum = jnp.sum(centre * centre, axis=0, keepdims=True)
    cross_sum = jnp.sum(centre * (d_hat - d_mean), axis=0, keepdims=True)
    rows = jnp.concatenate(
        [mean, spread_sum, d_mean, cross_sum, mean, spread_sum, d_mean, cross_sum], axis=0
    )
    for k in range(HEADS):
        stats_ref[k] = rows


def backward_kernel(recv_ref, att_ref, d_hat_ref, stats_ref, send_ref, d_query_ref):
    query = take(recv_ref, range(GROUPS), 2 * BLOCK, QUERIES)
    mask = allowed_mask()
    stats = [stats_ref[k] for k in range(HEADS)]

    def average(row):
        return sum(s[row : row + 1, :] for s in stats) / HEADS

    mean, d_mean = average(0), average(2)
    spread_mean = average(1) / HEAD_DIM + sum(
        (s[0:1, :] - mean) * (s[0:1, :] - mean) for s in stats
    ) / HEADS
    cross_mean = average(3) / HEAD_DIM + sum(
        (s[0:1, :] - mean) * (s[2:3, :] - d_mean) for s in stats
    ) / HEADS
    inv = lax.rsqrt(spread_mean + EPSILON)
    att = att_ref[...]
    att_hat = (att - mean) * inv
    d_att = (inv * (d_hat_ref[...] - d_mean - att_hat * (inv * cross_mean))).astype(BF16)
    out_att = att.T.astype(BF16)
    for j in range(4):
        key, value = span_keys(recv_ref, j)
        start = j * BLOCK
        half = dot_nt(key, query[start:, :]) * (0.5 * SCALE)
        th = jnp.tanh(half)
        weight = half + half * th
        slope = (0.5 * SCALE) * ((1.0 + th) + weight * (1.0 - th))
        d_score = dot(value, d_att[:, start:]) * slope

        def masked(values):
            first = jnp.where(mask, values[:, :BLOCK], 0.0)
            if j == 3:
                return first.astype(BF16)
            return jnp.concatenate([first, values[:, BLOCK:]], axis=1).astype(BF16)

        weight, d_score = masked(weight), masked(d_score)
        d_key = dot(d_score, query[start:, :]).astype(BF16)
        d_value = dot_nt(weight, d_att[:, start:]).astype(BF16)
        part = dot_tn(key, d_score)
        if j == 0:
            d_query_ref[...] = part
        else:
            d_query_ref[:, start:] += part
        for k in range(4):
            rows = slice(k * BLOCK, (k + 1) * BLOCK)
            send_ref[PLACE[4 * j + k], 0:BLOCK, :] = d_key[rows]
            send_ref[PLACE[4 * j + k], BLOCK : 2 * BLOCK, :] = d_value[rows]
    d_query = d_query_ref[...].T.astype(BF16)
    for c in range(GROUPS):
        rows = slice(c * QUERIES, (c + 1) * QUERIES)
        send_ref[PLACE[c], 2 * BLOCK : 2 * BLOCK + QUERIES, :] = d_query[rows]
        send_ref[PLACE[c], 2 * BLOCK + QUERIES :, :] = out_att[rows]


def collect(recv_ref, first, rows):
    return jnp.concatenate(
        [
            jnp.concatenate([recv_ref[PLACE[HEADS * g + h], first : first + rows, :] for g in range(HEADS)], axis=0)
            for h in range(HEADS)
        ],
        axis=1,
    ).astype(F32)


def collect_sum(recv_ref, first):
    def head(h):
        return sum(
            recv_ref[PLACE[HEADS * g + h], first : first + BLOCK, :].astype(F32) for g in range(HEADS)
        )

    return jnp.concatenate([head(h) for h in range(HEADS)], axis=1)


def finish_kernel(
    recv_ref,
    embedded_ref,
    gate_ref,
    slope_ref,
    d_gated_ref,
    upstream_ref,
    proj_in_ref,
    out_ref,
    gated_ref,
):
    att_hat = normalize(collect(recv_ref, 2 * BLOCK + QUERIES, QUERIES))[0]
    valid = valid_rows(d_gated_ref)
    gated_ref[...] = jnp.where(valid, att_hat * gate_ref[...].astype(F32), 0.0).astype(BF16)
    d_value = collect_sum(recv_ref, BLOCK) * slope_ref[:, WIDTH:]
    d_gate = d_gated_ref[:BLOCK, :] * att_hat * slope_ref[:, :WIDTH]
    d_query = collect(recv_ref, 2 * BLOCK, QUERIES)
    d_key = collect_sum(recv_ref, 0)
    d_normed = jnp.zeros((BLOCK, WIDTH), F32)
    for k, part in enumerate((d_gate, d_value, d_query, d_key)):
        d_normed += dot_nt(part.astype(BF16), proj_in_ref[:, k * WIDTH : (k + 1) * WIDTH])
    normed, inv_std = normalize(embedded_ref[...].astype(F32))
    d_embedded = upstream_ref[...].astype(F32) + norm_back(d_normed, normed, inv_std)
    d_embedded = jnp.where(valid, d_embedded, 0.0).astype(BF16)
    in_head, in_first, in_second = place_masks(d_gated_ref)
    half = WIDTH // 2
    out_ref[:, :WIDTH] = dot(in_head, d_embedded).astype(BF16)
    out_ref[:, WIDTH:] = (
        dot(in_first, d_embedded[:, :half]) + dot(in_second, d_embedded[:, half:])
    ).astype(BF16)


def scatter_kernel(wanted_ref, arrived_ref, out_ref):
    half = WIDTH // 2
    rest = arrived_ref[:, WIDTH:]
    row = (iota((SHARD_ROWS, SENT), 0) + 1).astype(F32)
    total = dot(one_hot(row == wanted_ref[0:1, :]), arrived_ref[:, :WIDTH])
    for k, start in enumerate((0, half)):
        tail = dot(one_hot(row == wanted_ref[k + 1 : k + 2, :]), rest)
        out_ref[:, start : start + half] = (total[:, start : start + half] + tail).astype(BF16)


def output_kernel(parts_ref, gated_ref, embedded_ref, proj_out_ref, grad_ref, out_ref):
    output = embedded_ref[...].astype(F32) + dot(gated_ref[...], proj_out_ref[...])
    out_ref[...] = output.astype(BF16)
    total = parts_ref[0].astype(F32)
    for k in range(1, GROUPS):
        total += parts_ref[k].astype(F32)
    grad_ref[...] = total


WHOLE = pl.BlockSpec(memory_space=pltpu.VMEM)


def run(kernel, name, outs, *args, scratch=(), vmem=40):
    single = not isinstance(outs, (list, tuple))
    return pl.pallas_call(
        kernel,
        out_shape=outs,
        in_specs=[WHOLE] * len(args),
        out_specs=WHOLE if single else [WHOLE] * len(outs),
        scratch_shapes=scratch,
        compiler_params=pltpu.CompilerParams(vmem_limit_bytes=vmem * 1024 * 1024),
        name=name,
    )(*args)


def shape(*dims, dtype=BF16):
    return jax.ShapeDtypeStruct(dims, dtype)


def swap(array, axis, groups=None):
    return lax.all_to_all(
        array, axis, split_axis=0, concat_axis=0, tiled=True, axis_index_groups=groups
    )


def local(item_ids, history_len, item_slot, table_slab, proj_in, proj_out, upstream):
    upstream = upstream[0]
    order = [[2 * ((3 * (p // 2)) % 16) + p % 2 for p in range(TABLES)]]
    requests, info = run(
        index_kernel,
        "index",
        [shape(TABLES, BLOCK, dtype=jnp.int32), shape(8, BLOCK, dtype=jnp.int32)],
        history_len.reshape(1, 1),
        item_ids,
        item_slot.reshape(BLOCK, BLOCK),
        vmem=60,
    )
    asked = swap(requests.reshape(TABLES, 1, BLOCK), "table", order)
    slab, d_gated = run(
        prepare_kernel,
        "prepare",
        [shape(SHARD_ROWS, WIDTH), shape(BLOCK + 8, WIDTH, dtype=F32)],
        table_slab,
        info,
        upstream,
        proj_out,
    )
    rows_out, wanted = run(
        gather_kernel, "gather", [shape(SENT, PACKED), shape(8, SENT, dtype=F32)], asked, slab
    )
    rows = swap(rows_out.reshape(TABLES, MAIN, PACKED), "table", order).reshape(SENT, PACKED)
    send, embedded, gate, slope = run(
        project_kernel,
        "project",
        [
            shape(GROUPS, PIECE, HEAD_DIM),
            shape(BLOCK, WIDTH),
            shape(BLOCK, WIDTH),
            shape(BLOCK, 2 * WIDTH, dtype=F32),
        ],
        rows,
        proj_in,
        d_gated,
    )
    recv = swap(send, "ctx", [ORDER])
    att, d_hat, stats = run(
        attend_kernel,
        "attend",
        [
            shape(HEAD_DIM, SPAN, dtype=F32),
            shape(HEAD_DIM, SPAN, dtype=F32),
            shape(HEADS, 8, SPAN, dtype=F32),
        ],
        recv,
    )
    lines = [[HEADS * g + h for h in range(HEADS)] for g in range(GROUPS // HEADS)]
    stats = swap(stats, "ctx", lines)
    send_back = run(
        backward_kernel,
        "backward",
        shape(GROUPS, PIECE, HEAD_DIM),
        recv,
        att,
        d_hat,
        stats,
        scratch=[pltpu.VMEM((HEAD_DIM, SPAN), F32)],
    )
    back = swap(send_back, "ctx", [ORDER])
    outgoing, gated = run(
        finish_kernel,
        "finish",
        [shape(SENT, PACKED), shape(BLOCK, WIDTH)],
        back,
        embedded,
        gate,
        slope,
        d_gated,
        upstream,
        proj_in,
    )
    arrived = swap(outgoing.reshape(TABLES, MAIN, PACKED), "table", order).reshape(SENT, PACKED)
    sums = run(scatter_kernel, "scatter", shape(SHARD_ROWS, WIDTH), wanted, arrived)
    parts = swap(sums.reshape(GROUPS, SHARD_ROWS // GROUPS, WIDTH), "ctx")
    table_grad, layer_out = run(
        output_kernel,
        "output",
        [shape(SHARD_ROWS // GROUPS, WIDTH, dtype=F32), shape(BLOCK, WIDTH)],
        parts,
        gated,
        embedded,
        proj_out,
    )
    return (layer_out[None], table_grad)


def solution(mesh):
    placed = (
        P("table", "ctx"),
        P("table"),
        P(),
        P("table", None),
        P(),
        P(),
        P("table", "ctx", None),
    )
    return jax.shard_map(
        local,
        mesh=mesh,
        in_specs=placed,
        out_specs=(P("table", "ctx", None), P(("table", "ctx"), None)),
        check_vma=False,
    )
```

```python
import jax
import jax.numpy as jnp
from jax import lax
from jax.experimental import pallas as pl
from jax.experimental.pallas import tpu as pltpu
from jax.sharding import PartitionSpec as P

EPSILON = 1e-05
BLOCK = 128
WIDTH = 512
HEADS = 4
HEAD_DIM = 128
TABLES = 32
GROUPS = 16
SHARD_ROWS = 512
QUERIES = BLOCK // HEADS
SEQ = BLOCK * GROUPS
SPAN = 4 * BLOCK
SCALE = HEAD_DIM ** (-0.5)
PIECE = 2 * BLOCK + 2 * QUERIES
MAIN = 8
SENT = TABLES * MAIN
PACKED = WIDTH + WIDTH // 2
ORDER = [0, 1, 2, 3, 7, 6, 5, 4, 8, 9, 10, 11, 15, 14, 13, 12]
PLACE = [ORDER.index(c) for c in range(GROUPS)]

F32 = jnp.float32
BF16 = jnp.bfloat16


def dot(a, b):
    return jnp.dot(a, b, preferred_element_type=F32)


def dot_nt(a, b):
    return lax.dot_general(a, b, (((1,), (1,)), ((), ())), preferred_element_type=F32)


def dot_tn(a, b):
    return lax.dot_general(a, b, (((0,), (0,)), ((), ())), preferred_element_type=F32)


def iota(shape, dim):
    return lax.broadcasted_iota(jnp.int32, shape, dim)


def one_hot(mask):
    return jnp.where(mask, 1.0, 0.0).astype(BF16)


def normalize(values):
    centre = values - jnp.mean(values, axis=-1, keepdims=True)
    scale_inv = lax.rsqrt(jnp.mean(centre * centre, axis=-1, keepdims=True) + EPSILON)
    return (centre * scale_inv, scale_inv)


def silu_and_slope(values):
    half = 0.5 * values
    th = jnp.tanh(half)
    out = half + half * th
    return out, 0.5 * ((1.0 + th) + out * (1.0 - th))


def norm_back(grad, normed, scale_inv):
    return scale_inv * (
        grad
        - jnp.mean(grad, axis=-1, keepdims=True)
        - normed * jnp.mean(grad * normed, axis=-1, keepdims=True)
    )


def index_kernel(length_ref, ids_ref, slot_ref, send_ref, info_ref):
    ids = ids_ref[...]
    event = iota((1, BLOCK), 1)
    length = length_ref[...]
    valid = lax.axis_index("ctx") * BLOCK + event < length
    row = iota((BLOCK, BLOCK), 0)
    table = slot_ref[...]
    rows_hot = one_hot(row == (ids >> 7))
    high = dot_tn((table >> 7).astype(F32).astype(BF16), rows_hot)
    low = dot_tn((table & 127).astype(F32).astype(BF16), rows_hot)
    both = jnp.where(row == (ids & 127), high * 128.0 + low, 0.0)
    slots = jnp.sum(both, axis=0, keepdims=True).astype(jnp.int32)
    shard = slots >> 9
    owner = jnp.where(valid, 2 * (4 * ((((shard >> 1) & 3) - (3 - ((shard >> 1) >> 2))) & 3) + 3 - ((shard >> 1) >> 2)) + (shard & 1), TABLES)
    wanted = (slots & (SHARD_ROWS - 1)) + 1
    owned = iota((TABLES, BLOCK), 0) == owner
    owned_hot = one_hot(owned)
    earlier = dot(owned_hot, one_hot(row < iota((BLOCK, BLOCK), 1)))
    rank = jnp.sum(jnp.where(owned, earlier, 0.0), axis=0, keepdims=True).astype(jnp.int32)
    head = jnp.where(valid & (rank < MAIN), owner * MAIN + rank, -1000)
    tail = jnp.where(valid & (rank >= MAIN), owner * MAIN + rank - MAIN, -1000)
    lengths = jnp.broadcast_to(length, (6, BLOCK))
    info_ref[...] = jnp.concatenate([head, tail, lengths], axis=0)
    ranked = jnp.where(row < BLOCK // 2, row & 7, MAIN + (row & 3)) == rank
    wanted_high = jnp.where(ranked, (wanted >> 5).astype(F32), 0.0).astype(BF16)
    wanted_low = jnp.where(ranked, (wanted & 31).astype(F32), 0.0).astype(BF16)
    asked = dot_nt(owned_hot, wanted_high) * 32.0 + dot_nt(owned_hot, wanted_low)
    send_ref[...] = asked.astype(jnp.int32)


def asked_rows(asked_ref):
    asked = asked_ref[...].reshape(TABLES, BLOCK).astype(F32)
    turned = pltpu.roll(asked, BLOCK // 2, 1)
    left = iota((TABLES, BLOCK), 1) < BLOCK // 2
    both = []
    for wanted in (jnp.where(left, asked, turned), jnp.where(left, turned, asked)):
        parts = []
        for k in range(SENT // BLOCK):
            own = iota((TABLES, BLOCK), 0) == (iota((TABLES, BLOCK), 1) >> 3) + k * BLOCK // MAIN
            parts.append(jnp.sum(jnp.where(own, wanted, 0.0), axis=0, keepdims=True))
        both.append(jnp.concatenate(parts, axis=1))
    return both


def gather_kernel(asked_ref, slab_ref, out_ref, rows_ref):
    head, tail = asked_rows(asked_ref)
    first = (iota((1, SENT), 1) & 7) < 4
    tail_first = jnp.where(first, tail, 0.0)
    tail_second = jnp.where(first, 0.0, tail)
    rows_ref[...] = jnp.concatenate(
        [head, tail_first, tail_second, head, tail_first, tail_second, head, tail], axis=0
    )
    half = WIDTH // 2
    row = (iota((SHARD_ROWS, SENT), 0) + 1).astype(F32)
    out_ref[:, :WIDTH] = dot_tn(one_hot(row == head), slab_ref[...]).astype(BF16)
    rest = dot_tn(one_hot(row == tail_first), slab_ref[:, :half])
    rest += dot_tn(one_hot(row == tail_second), slab_ref[:, half:])
    out_ref[:, WIDTH:] = rest.astype(BF16)


def valid_rows(d_gated_ref):
    length = d_gated_ref[BLOCK + 2 : BLOCK + 3, 0:1].astype(jnp.int32)
    return lax.axis_index("ctx") * BLOCK + iota((BLOCK, WIDTH), 0) < length


def place_masks(d_gated_ref):
    place = iota((SENT, BLOCK), 0)
    head = d_gated_ref[BLOCK : BLOCK + 1, :BLOCK].astype(jnp.int32)
    tail = d_gated_ref[BLOCK + 1 : BLOCK + 2, :BLOCK].astype(jnp.int32)
    return one_hot(place == head), one_hot(place == tail), one_hot(place == tail + 4)


def prepare_kernel(slab_ref, info_ref, upstream_ref, proj_out_ref, narrow_ref, d_gated_ref):
    narrow_ref[...] = slab_ref[...].astype(BF16)
    place = lax.axis_index("ctx") * BLOCK + iota((BLOCK, WIDTH), 0)
    d_out = jnp.where(place < info_ref[2:3, 0:1], upstream_ref[...], jnp.zeros((), BF16))
    d_gated_ref[:BLOCK, :] = dot_nt(d_out, proj_out_ref[...])
    d_gated_ref[BLOCK:, :BLOCK] = info_ref[...].astype(F32)
    d_gated_ref[BLOCK:, BLOCK:] = jnp.zeros((8, WIDTH - BLOCK), F32)


def project_kernel(
    rows_ref, proj_in_ref, d_gated_ref, send_ref, embedded_ref, gate_ref, slope_ref
):
    in_head, in_first, in_second = place_masks(d_gated_ref)
    half = WIDTH // 2
    rest = rows_ref[:, WIDTH:]
    embedded = dot_tn(in_head, rows_ref[:, :WIDTH]) + jnp.concatenate(
        [dot_tn(in_first, rest), dot_tn(in_second, rest)], axis=1
    )
    valid = valid_rows(d_gated_ref)
    embedded = jnp.where(valid, embedded, 0.0)
    embedded_ref[...] = embedded.astype(BF16)
    normed = normalize(embedded)[0].astype(BF16)

    def part(k):
        return dot(normed, proj_in_ref[:, k * WIDTH : (k + 1) * WIDTH])

    gate_part = part(0)
    value_part = part(1)
    gate, slope_ref[:, :WIDTH] = silu_and_slope(gate_part)
    value, slope_ref[:, WIDTH:] = silu_and_slope(value_part)
    gate, value = gate.astype(BF16), value.astype(BF16)
    gate_ref[...] = gate
    value = jnp.where(valid, value, jnp.zeros((), BF16))
    query = part(2).astype(BF16)
    key = jnp.where(valid, part(3), 0.0).astype(BF16)
    d_hat = (d_gated_ref[:BLOCK, :] * gate.astype(F32)).astype(BF16)
    for h in range(HEADS):
        cols = slice(h * HEAD_DIM, (h + 1) * HEAD_DIM)
        for g in range(HEADS):
            rows = slice(g * QUERIES, (g + 1) * QUERIES)
            chunk = PLACE[HEADS * g + h]
            send_ref[chunk, 0:BLOCK, :] = key[:, cols]
            send_ref[chunk, BLOCK : 2 * BLOCK, :] = value[:, cols]
            send_ref[chunk, 2 * BLOCK : 2 * BLOCK + QUERIES, :] = query[rows, cols]
            send_ref[chunk, 2 * BLOCK + QUERIES :, :] = d_hat[rows, cols]


def allowed_mask():
    group = lax.axis_index("ctx") // HEADS
    lane = iota((SPAN, BLOCK), 1)
    place = (lane // QUERIES) * BLOCK + group * QUERIES + lane % QUERIES
    return iota((SPAN, BLOCK), 0) <= place


def take(recv_ref, blocks, first, rows):
    return jnp.concatenate([recv_ref[PLACE[c], first : first + rows, :] for c in blocks], axis=0)


def span_keys(recv_ref, j):
    blocks = range(4 * j, 4 * j + 4)
    return take(recv_ref, blocks, 0, BLOCK), take(recv_ref, blocks, BLOCK, BLOCK)


def attend_kernel(recv_ref, att_ref, d_hat_ref, stats_ref):
    query = take(recv_ref, range(GROUPS), 2 * BLOCK, QUERIES)
    mask = allowed_mask()
    for j in range(4):
        key, value = span_keys(recv_ref, j)
        start = j * BLOCK
        parts = []
        for k in range(0, SPAN, SPAN // 2):
            rows = slice(k, k + SPAN // 2)
            half = dot_nt(key[rows], query[start:, :]) * (0.5 * SCALE)
            weight = half + half * jnp.tanh(half)
            first = jnp.where(mask[rows], weight[:, :BLOCK], 0.0)
            if j < 3:
                first = jnp.concatenate([first, weight[:, BLOCK:]], axis=1)
            parts.append(first.astype(BF16))
        part = dot_tn(value, jnp.concatenate(parts, axis=0))
        if j == 0:
            att_ref[...] = part
        else:
            att_ref[:, start:] += part
    d_hat = take(recv_ref, range(GROUPS), 2 * BLOCK + QUERIES, QUERIES)
    d_hat = d_hat.astype(F32).T
    d_hat_ref[...] = d_hat
    att = att_ref[...]
    mean = jnp.mean(att, axis=0, keepdims=True)
    centre = att - mean
    d_mean = jnp.mean(d_hat, axis=0, keepdims=True)
    spread_sum = jnp.sum(centre * centre, axis=0, keepdims=True)
    cross_sum = jnp.sum(centre * (d_hat - d_mean), axis=0, keepdims=True)
    rows = jnp.concatenate([mean, spread_sum, d_mean, cross_sum], axis=0)
    for k in range(HEADS):
        stats_ref[k] = rows


def backward_kernel(recv_ref, att_ref, d_hat_ref, stats_ref, send_ref, d_query_ref):
    query = take(recv_ref, range(GROUPS), 2 * BLOCK, QUERIES)
    mask = allowed_mask()
    stats = [stats_ref[k] for k in range(HEADS)]

    def average(row):
        return sum(s[row : row + 1, :] for s in stats) / HEADS

    mean, d_mean = average(0), average(2)
    spread_mean = average(1) / HEAD_DIM + sum(
        (s[0:1, :] - mean) * (s[0:1, :] - mean) for s in stats
    ) / HEADS
    cross_mean = average(3) / HEAD_DIM + sum(
        (s[0:1, :] - mean) * (s[2:3, :] - d_mean) for s in stats
    ) / HEADS
    inv = lax.rsqrt(spread_mean + EPSILON)
    att = att_ref[...]
    att_hat = (att - mean) * inv
    d_att = (inv * (d_hat_ref[...] - d_mean - att_hat * (inv * cross_mean))).astype(BF16)
    out_att = att.T.astype(BF16)
    for j in range(4):
        key, value = span_keys(recv_ref, j)
        start = j * BLOCK
        half = dot_nt(key, query[start:, :]) * (0.5 * SCALE)
        th = jnp.tanh(half)
        weight = half + half * th
        slope = (0.5 * SCALE) * ((1.0 + th) + weight * (1.0 - th))
        d_score = dot(value, d_att[:, start:]) * slope

        def masked(values):
            first = jnp.where(mask, values[:, :BLOCK], 0.0)
            if j == 3:
                return first.astype(BF16)
            return jnp.concatenate([first, values[:, BLOCK:]], axis=1).astype(BF16)

        weight, d_score = masked(weight), masked(d_score)
        d_key = dot(d_score, query[start:, :]).astype(BF16)
        d_value = dot_nt(weight, d_att[:, start:]).astype(BF16)
        part = dot_tn(key, d_score)
        if j == 0:
            d_query_ref[...] = part
        else:
            d_query_ref[:, start:] += part
        for k in range(4):
            rows = slice(k * BLOCK, (k + 1) * BLOCK)
            send_ref[PLACE[4 * j + k], 0:BLOCK, :] = d_key[rows]
            send_ref[PLACE[4 * j + k], BLOCK : 2 * BLOCK, :] = d_value[rows]
    d_query = d_query_ref[...].T.astype(BF16)
    for c in range(GROUPS):
        rows = slice(c * QUERIES, (c + 1) * QUERIES)
        send_ref[PLACE[c], 2 * BLOCK : 2 * BLOCK + QUERIES, :] = d_query[rows]
        send_ref[PLACE[c], 2 * BLOCK + QUERIES :, :] = out_att[rows]


def collect(recv_ref, first, rows):
    return jnp.concatenate(
        [
            jnp.concatenate([recv_ref[PLACE[HEADS * g + h], first : first + rows, :] for g in range(HEADS)], axis=0)
            for h in range(HEADS)
        ],
        axis=1,
    ).astype(F32)


def collect_sum(recv_ref, first):
    def head(h):
        return sum(
            recv_ref[PLACE[HEADS * g + h], first : first + BLOCK, :].astype(F32) for g in range(HEADS)
        )

    return jnp.concatenate([head(h) for h in range(HEADS)], axis=1)


def finish_kernel(
    recv_ref,
    embedded_ref,
    gate_ref,
    slope_ref,
    d_gated_ref,
    upstream_ref,
    proj_in_ref,
    out_ref,
    gated_ref,
):
    att_hat = normalize(collect(recv_ref, 2 * BLOCK + QUERIES, QUERIES))[0]
    valid = valid_rows(d_gated_ref)
    gated_ref[...] = jnp.where(valid, att_hat * gate_ref[...].astype(F32), 0.0).astype(BF16)
    d_value = collect_sum(recv_ref, BLOCK) * slope_ref[:, WIDTH:]
    d_gate = d_gated_ref[:BLOCK, :] * att_hat * slope_ref[:, :WIDTH]
    d_query = collect(recv_ref, 2 * BLOCK, QUERIES)
    d_key = collect_sum(recv_ref, 0)
    d_normed = jnp.zeros((BLOCK, WIDTH), F32)
    for k, part in enumerate((d_gate, d_value, d_query, d_key)):
        d_normed += dot_nt(part.astype(BF16), proj_in_ref[:, k * WIDTH : (k + 1) * WIDTH])
    normed, inv_std = normalize(embedded_ref[...].astype(F32))
    d_embedded = upstream_ref[...].astype(F32) + norm_back(d_normed, normed, inv_std)
    d_embedded = jnp.where(valid, d_embedded, 0.0).astype(BF16)
    in_head, in_first, in_second = place_masks(d_gated_ref)
    half = WIDTH // 2
    out_ref[:, :WIDTH] = dot(in_head, d_embedded).astype(BF16)
    out_ref[:, WIDTH:] = (
        dot(in_first, d_embedded[:, :half]) + dot(in_second, d_embedded[:, half:])
    ).astype(BF16)


def scatter_kernel(wanted_ref, arrived_ref, out_ref):
    half = WIDTH // 2
    rest = arrived_ref[:, WIDTH:]
    row = (iota((SHARD_ROWS, SENT), 0) + 1).astype(F32)
    total = dot(one_hot(row == wanted_ref[0:1, :]), arrived_ref[:, :WIDTH])
    for k, start in enumerate((0, half)):
        tail = dot(one_hot(row == wanted_ref[k + 1 : k + 2, :]), rest)
        out_ref[:, start : start + half] = (total[:, start : start + half] + tail).astype(BF16)


def output_kernel(parts_ref, gated_ref, embedded_ref, proj_out_ref, grad_ref, out_ref):
    output = embedded_ref[...].astype(F32) + dot(gated_ref[...], proj_out_ref[...])
    out_ref[...] = output.astype(BF16)
    total = parts_ref[0].astype(F32)
    for k in range(1, GROUPS):
        total += parts_ref[k].astype(F32)
    grad_ref[...] = total


WHOLE = pl.BlockSpec(memory_space=pltpu.VMEM)


def run(kernel, name, outs, *args, scratch=(), vmem=40):
    single = not isinstance(outs, (list, tuple))
    return pl.pallas_call(
        kernel,
        out_shape=outs,
        in_specs=[WHOLE] * len(args),
        out_specs=WHOLE if single else [WHOLE] * len(outs),
        scratch_shapes=scratch,
        compiler_params=pltpu.CompilerParams(vmem_limit_bytes=vmem * 1024 * 1024),
        name=name,
    )(*args)


def shape(*dims, dtype=BF16):
    return jax.ShapeDtypeStruct(dims, dtype)


def swap(array, axis, groups=None):
    return lax.all_to_all(
        array, axis, split_axis=0, concat_axis=0, tiled=True, axis_index_groups=groups
    )


def local(item_ids, history_len, item_slot, table_slab, proj_in, proj_out, upstream):
    upstream = upstream[0]
    order = [[2 * (4 * (3 - (p // 2) % 4) + ((p // 2) // 4 + (p // 2) % 4) % 4) + p % 2 for p in range(TABLES)]]
    requests, info = run(
        index_kernel,
        "index",
        [shape(TABLES, BLOCK, dtype=jnp.int32), shape(8, BLOCK, dtype=jnp.int32)],
        history_len.reshape(1, 1),
        item_ids,
        item_slot.reshape(BLOCK, BLOCK),
        vmem=60,
    )
    asked = swap(requests.reshape(TABLES, 1, BLOCK), "table", order)
    slab, d_gated = run(
        prepare_kernel,
        "prepare",
        [shape(SHARD_ROWS, WIDTH), shape(BLOCK + 8, WIDTH, dtype=F32)],
        table_slab,
        info,
        upstream,
        proj_out,
    )
    rows_out, wanted = run(
        gather_kernel, "gather", [shape(SENT, PACKED), shape(8, SENT, dtype=F32)], asked, slab
    )
    rows = swap(rows_out.reshape(TABLES, MAIN, PACKED), "table", order).reshape(SENT, PACKED)
    send, embedded, gate, slope = run(
        project_kernel,
        "project",
        [
            shape(GROUPS, PIECE, HEAD_DIM),
            shape(BLOCK, WIDTH),
            shape(BLOCK, WIDTH),
            shape(BLOCK, 2 * WIDTH, dtype=F32),
        ],
        rows,
        proj_in,
        d_gated,
    )
    recv = swap(send, "ctx", [ORDER])
    att, d_hat, stats = run(
        attend_kernel,
        "attend",
        [
            shape(HEAD_DIM, SPAN, dtype=F32),
            shape(HEAD_DIM, SPAN, dtype=F32),
            shape(HEADS, 4, SPAN, dtype=F32),
        ],
        recv,
    )
    lines = [[HEADS * g + h for h in range(HEADS)] for g in range(GROUPS // HEADS)]
    stats = swap(stats, "ctx", lines)
    send_back = run(
        backward_kernel,
        "backward",
        shape(GROUPS, PIECE, HEAD_DIM),
        recv,
        att,
        d_hat,
        stats,
        scratch=[pltpu.VMEM((HEAD_DIM, SPAN), F32)],
    )
    back = swap(send_back, "ctx", [ORDER])
    outgoing, gated = run(
        finish_kernel,
        "finish",
        [shape(SENT, PACKED), shape(BLOCK, WIDTH)],
        back,
        embedded,
        gate,
        slope,
        d_gated,
        upstream,
        proj_in,
    )
    arrived = swap(outgoing.reshape(TABLES, MAIN, PACKED), "table", order).reshape(SENT, PACKED)
    sums = run(scatter_kernel, "scatter", shape(SHARD_ROWS, WIDTH), wanted, arrived)
    parts = swap(sums.reshape(GROUPS, SHARD_ROWS // GROUPS, WIDTH), "ctx")
    table_grad, layer_out = run(
        output_kernel,
        "output",
        [shape(SHARD_ROWS // GROUPS, WIDTH, dtype=F32), shape(BLOCK, WIDTH)],
        parts,
        gated,
        embedded,
        proj_out,
    )
    return (layer_out[None], table_grad)


def solution(mesh):
    placed = (
        P("table", "ctx"),
        P("table"),
        P(),
        P("table", None),
        P(),
        P(),
        P("table", "ctx", None),
    )
    return jax.shard_map(
        local,
        mesh=mesh,
        in_specs=placed,
        out_specs=(P("table", "ctx", None), P(("table", "ctx"), None)),
        check_vma=False,
    )
```

```python
import jax
import jax.numpy as jnp
from jax import lax
from jax.experimental import pallas as pl
from jax.experimental.pallas import tpu as pltpu
from jax.sharding import PartitionSpec as P

EPSILON = 1e-05
BLOCK = 128
WIDTH = 512
HEADS = 4
HEAD_DIM = 128
TABLES = 32
GROUPS = 16
SHARD_ROWS = 512
QUERIES = BLOCK // HEADS
SEQ = BLOCK * GROUPS
SPAN = 4 * BLOCK
SCALE = HEAD_DIM ** (-0.5)
PIECE = 2 * BLOCK + 2 * QUERIES
MAIN = 8
SENT = TABLES * MAIN
PACKED = WIDTH + WIDTH // 2
ORDER = [0, 1, 2, 3, 7, 6, 5, 4, 8, 9, 10, 11, 15, 14, 13, 12]
PLACE = [ORDER.index(c) for c in range(GROUPS)]

F32 = jnp.float32
BF16 = jnp.bfloat16


def dot(a, b):
    return jnp.dot(a, b, preferred_element_type=F32)


def dot_nt(a, b):
    return lax.dot_general(a, b, (((1,), (1,)), ((), ())), preferred_element_type=F32)


def dot_tn(a, b):
    return lax.dot_general(a, b, (((0,), (0,)), ((), ())), preferred_element_type=F32)


def iota(shape, dim):
    return lax.broadcasted_iota(jnp.int32, shape, dim)


def one_hot(mask):
    return jnp.where(mask, 1.0, 0.0).astype(BF16)


def normalize(values):
    centre = values - jnp.mean(values, axis=-1, keepdims=True)
    scale_inv = lax.rsqrt(jnp.mean(centre * centre, axis=-1, keepdims=True) + EPSILON)
    return (centre * scale_inv, scale_inv)


def silu_and_slope(values):
    half = 0.5 * values
    th = jnp.tanh(half)
    out = half + half * th
    return out, 0.5 * ((1.0 + th) + out * (1.0 - th))


def norm_back(grad, normed, scale_inv):
    return scale_inv * (
        grad
        - jnp.mean(grad, axis=-1, keepdims=True)
        - normed * jnp.mean(grad * normed, axis=-1, keepdims=True)
    )


def index_kernel(length_ref, ids_ref, slot_ref, send_ref, info_ref):
    ids = ids_ref[...]
    event = iota((1, BLOCK), 1)
    length = length_ref[...]
    valid = lax.axis_index("ctx") * BLOCK + event < length
    row = iota((BLOCK, BLOCK), 0)
    table = slot_ref[...]
    rows_hot = one_hot(row == (ids >> 7))
    high = dot_tn((table >> 7).astype(F32).astype(BF16), rows_hot)
    low = dot_tn((table & 127).astype(F32).astype(BF16), rows_hot)
    both = jnp.where(row == (ids & 127), high * 128.0 + low, 0.0)
    slots = jnp.sum(both, axis=0, keepdims=True).astype(jnp.int32)
    shard = slots >> 9
    owner = jnp.where(valid, 2 * (4 * ((((shard >> 1) & 3) - 3 * (3 - ((shard >> 1) >> 2))) & 3) + 3 - ((shard >> 1) >> 2)) + (shard & 1), TABLES)
    wanted = (slots & (SHARD_ROWS - 1)) + 1
    owned = iota((TABLES, BLOCK), 0) == owner
    owned_hot = one_hot(owned)
    earlier = dot(owned_hot, one_hot(row < iota((BLOCK, BLOCK), 1)))
    rank = jnp.sum(jnp.where(owned, earlier, 0.0), axis=0, keepdims=True).astype(jnp.int32)
    head = jnp.where(valid & (rank < MAIN), owner * MAIN + rank, -1000)
    tail = jnp.where(valid & (rank >= MAIN), owner * MAIN + rank - MAIN, -1000)
    lengths = jnp.broadcast_to(length, (6, BLOCK))
    info_ref[...] = jnp.concatenate([head, tail, lengths], axis=0)
    ranked = jnp.where(row < BLOCK // 2, row & 7, MAIN + (row & 3)) == rank
    wanted_high = jnp.where(ranked, (wanted >> 5).astype(F32), 0.0).astype(BF16)
    wanted_low = jnp.where(ranked, (wanted & 31).astype(F32), 0.0).astype(BF16)
    asked = dot_nt(owned_hot, wanted_high) * 32.0 + dot_nt(owned_hot, wanted_low)
    send_ref[...] = asked.astype(jnp.int32)


def asked_rows(asked_ref):
    asked = asked_ref[...].reshape(TABLES, BLOCK).astype(F32)
    turned = pltpu.roll(asked, BLOCK // 2, 1)
    left = iota((TABLES, BLOCK), 1) < BLOCK // 2
    both = []
    for wanted in (jnp.where(left, asked, turned), jnp.where(left, turned, asked)):
        parts = []
        for k in range(SENT // BLOCK):
            own = iota((TABLES, BLOCK), 0) == (iota((TABLES, BLOCK), 1) >> 3) + k * BLOCK // MAIN
            parts.append(jnp.sum(jnp.where(own, wanted, 0.0), axis=0, keepdims=True))
        both.append(jnp.concatenate(parts, axis=1))
    return both


def gather_kernel(asked_ref, slab_ref, out_ref, rows_ref):
    head, tail = asked_rows(asked_ref)
    first = (iota((1, SENT), 1) & 7) < 4
    tail_first = jnp.where(first, tail, 0.0)
    tail_second = jnp.where(first, 0.0, tail)
    rows_ref[...] = jnp.concatenate(
        [head, tail_first, tail_second, head, tail_first, tail_second, head, tail], axis=0
    )
    half = WIDTH // 2
    row = (iota((SHARD_ROWS, SENT), 0) + 1).astype(F32)
    out_ref[:, :WIDTH] = dot_tn(one_hot(row == head), slab_ref[...]).astype(BF16)
    rest = dot_tn(one_hot(row == tail_first), slab_ref[:, :half])
    rest += dot_tn(one_hot(row == tail_second), slab_ref[:, half:])
    out_ref[:, WIDTH:] = rest.astype(BF16)


def valid_rows(d_gated_ref):
    length = d_gated_ref[BLOCK + 2 : BLOCK + 3, 0:1].astype(jnp.int32)
    return lax.axis_index("ctx") * BLOCK + iota((BLOCK, WIDTH), 0) < length


def place_masks(d_gated_ref):
    place = iota((SENT, BLOCK), 0)
    head = d_gated_ref[BLOCK : BLOCK + 1, :BLOCK].astype(jnp.int32)
    tail = d_gated_ref[BLOCK + 1 : BLOCK + 2, :BLOCK].astype(jnp.int32)
    return one_hot(place == head), one_hot(place == tail), one_hot(place == tail + 4)


def prepare_kernel(slab_ref, info_ref, upstream_ref, proj_out_ref, narrow_ref, d_gated_ref):
    narrow_ref[...] = slab_ref[...].astype(BF16)
    place = lax.axis_index("ctx") * BLOCK + iota((BLOCK, WIDTH), 0)
    d_out = jnp.where(place < info_ref[2:3, 0:1], upstream_ref[...], jnp.zeros((), BF16))
    d_gated_ref[:BLOCK, :] = dot_nt(d_out, proj_out_ref[...])
    d_gated_ref[BLOCK:, :BLOCK] = info_ref[...].astype(F32)
    d_gated_ref[BLOCK:, BLOCK:] = jnp.zeros((8, WIDTH - BLOCK), F32)


def project_kernel(
    rows_ref, proj_in_ref, d_gated_ref, send_ref, embedded_ref, gate_ref, slope_ref
):
    in_head, in_first, in_second = place_masks(d_gated_ref)
    half = WIDTH // 2
    rest = rows_ref[:, WIDTH:]
    embedded = dot_tn(in_head, rows_ref[:, :WIDTH]) + jnp.concatenate(
        [dot_tn(in_first, rest), dot_tn(in_second, rest)], axis=1
    )
    valid = valid_rows(d_gated_ref)
    embedded = jnp.where(valid, embedded, 0.0)
    embedded_ref[...] = embedded.astype(BF16)
    normed = normalize(embedded)[0].astype(BF16)

    def part(k):
        return dot(normed, proj_in_ref[:, k * WIDTH : (k + 1) * WIDTH])

    gate_part = part(0)
    value_part = part(1)
    gate, slope_ref[:, :WIDTH] = silu_and_slope(gate_part)
    value, slope_ref[:, WIDTH:] = silu_and_slope(value_part)
    gate, value = gate.astype(BF16), value.astype(BF16)
    gate_ref[...] = gate
    value = jnp.where(valid, value, jnp.zeros((), BF16))
    query = part(2).astype(BF16)
    key = jnp.where(valid, part(3), 0.0).astype(BF16)
    d_hat = (d_gated_ref[:BLOCK, :] * gate.astype(F32)).astype(BF16)
    for h in range(HEADS):
        cols = slice(h * HEAD_DIM, (h + 1) * HEAD_DIM)
        for g in range(HEADS):
            rows = slice(g * QUERIES, (g + 1) * QUERIES)
            chunk = PLACE[HEADS * g + h]
            send_ref[chunk, 0:BLOCK, :] = key[:, cols]
            send_ref[chunk, BLOCK : 2 * BLOCK, :] = value[:, cols]
            send_ref[chunk, 2 * BLOCK : 2 * BLOCK + QUERIES, :] = query[rows, cols]
            send_ref[chunk, 2 * BLOCK + QUERIES :, :] = d_hat[rows, cols]


def allowed_mask():
    group = lax.axis_index("ctx") // HEADS
    lane = iota((SPAN, BLOCK), 1)
    place = (lane // QUERIES) * BLOCK + group * QUERIES + lane % QUERIES
    return iota((SPAN, BLOCK), 0) <= place


def take(recv_ref, blocks, first, rows):
    return jnp.concatenate([recv_ref[PLACE[c], first : first + rows, :] for c in blocks], axis=0)


def span_keys(recv_ref, j):
    blocks = range(4 * j, 4 * j + 4)
    return take(recv_ref, blocks, 0, BLOCK), take(recv_ref, blocks, BLOCK, BLOCK)


def attend_kernel(recv_ref, att_ref, d_hat_ref, stats_ref):
    query = take(recv_ref, range(GROUPS), 2 * BLOCK, QUERIES)
    mask = allowed_mask()
    for j in range(4):
        key, value = span_keys(recv_ref, j)
        start = j * BLOCK
        parts = []
        for k in range(0, SPAN, SPAN // 2):
            rows = slice(k, k + SPAN // 2)
            half = dot_nt(key[rows], query[start:, :]) * (0.5 * SCALE)
            weight = half + half * jnp.tanh(half)
            first = jnp.where(mask[rows], weight[:, :BLOCK], 0.0)
            if j < 3:
                first = jnp.concatenate([first, weight[:, BLOCK:]], axis=1)
            parts.append(first.astype(BF16))
        part = dot_tn(value, jnp.concatenate(parts, axis=0))
        if j == 0:
            att_ref[...] = part
        else:
            att_ref[:, start:] += part
    d_hat = take(recv_ref, range(GROUPS), 2 * BLOCK + QUERIES, QUERIES)
    d_hat = d_hat.astype(F32).T
    d_hat_ref[...] = d_hat
    att = att_ref[...]
    mean = jnp.mean(att, axis=0, keepdims=True)
    centre = att - mean
    d_mean = jnp.mean(d_hat, axis=0, keepdims=True)
    spread_sum = jnp.sum(centre * centre, axis=0, keepdims=True)
    cross_sum = jnp.sum(centre * (d_hat - d_mean), axis=0, keepdims=True)
    rows = jnp.concatenate([mean, spread_sum, d_mean, cross_sum], axis=0)
    for k in range(HEADS):
        stats_ref[k] = rows


def backward_kernel(recv_ref, att_ref, d_hat_ref, stats_ref, send_ref, d_query_ref):
    query = take(recv_ref, range(GROUPS), 2 * BLOCK, QUERIES)
    mask = allowed_mask()
    stats = [stats_ref[k] for k in range(HEADS)]

    def average(row):
        return sum(s[row : row + 1, :] for s in stats) / HEADS

    mean, d_mean = average(0), average(2)
    spread_mean = average(1) / HEAD_DIM + sum(
        (s[0:1, :] - mean) * (s[0:1, :] - mean) for s in stats
    ) / HEADS
    cross_mean = average(3) / HEAD_DIM + sum(
        (s[0:1, :] - mean) * (s[2:3, :] - d_mean) for s in stats
    ) / HEADS
    inv = lax.rsqrt(spread_mean + EPSILON)
    att = att_ref[...]
    att_hat = (att - mean) * inv
    d_att = (inv * (d_hat_ref[...] - d_mean - att_hat * (inv * cross_mean))).astype(BF16)
    out_att = att.T.astype(BF16)
    for j in range(4):
        key, value = span_keys(recv_ref, j)
        start = j * BLOCK
        half = dot_nt(key, query[start:, :]) * (0.5 * SCALE)
        th = jnp.tanh(half)
        weight = half + half * th
        slope = (0.5 * SCALE) * ((1.0 + th) + weight * (1.0 - th))
        d_score = dot(value, d_att[:, start:]) * slope

        def masked(values):
            first = jnp.where(mask, values[:, :BLOCK], 0.0)
            if j == 3:
                return first.astype(BF16)
            return jnp.concatenate([first, values[:, BLOCK:]], axis=1).astype(BF16)

        weight, d_score = masked(weight), masked(d_score)
        d_key = dot(d_score, query[start:, :]).astype(BF16)
        d_value = dot_nt(weight, d_att[:, start:]).astype(BF16)
        part = dot_tn(key, d_score)
        if j == 0:
            d_query_ref[...] = part
        else:
            d_query_ref[:, start:] += part
        for k in range(4):
            rows = slice(k * BLOCK, (k + 1) * BLOCK)
            send_ref[PLACE[4 * j + k], 0:BLOCK, :] = d_key[rows]
            send_ref[PLACE[4 * j + k], BLOCK : 2 * BLOCK, :] = d_value[rows]
    d_query = d_query_ref[...].T.astype(BF16)
    for c in range(GROUPS):
        rows = slice(c * QUERIES, (c + 1) * QUERIES)
        send_ref[PLACE[c], 2 * BLOCK : 2 * BLOCK + QUERIES, :] = d_query[rows]
        send_ref[PLACE[c], 2 * BLOCK + QUERIES :, :] = out_att[rows]


def collect(recv_ref, first, rows):
    return jnp.concatenate(
        [
            jnp.concatenate([recv_ref[PLACE[HEADS * g + h], first : first + rows, :] for g in range(HEADS)], axis=0)
            for h in range(HEADS)
        ],
        axis=1,
    ).astype(F32)


def collect_sum(recv_ref, first):
    def head(h):
        return sum(
            recv_ref[PLACE[HEADS * g + h], first : first + BLOCK, :].astype(F32) for g in range(HEADS)
        )

    return jnp.concatenate([head(h) for h in range(HEADS)], axis=1)


def finish_kernel(
    recv_ref,
    embedded_ref,
    gate_ref,
    slope_ref,
    d_gated_ref,
    upstream_ref,
    proj_in_ref,
    out_ref,
    gated_ref,
):
    att_hat = normalize(collect(recv_ref, 2 * BLOCK + QUERIES, QUERIES))[0]
    valid = valid_rows(d_gated_ref)
    gated_ref[...] = jnp.where(valid, att_hat * gate_ref[...].astype(F32), 0.0).astype(BF16)
    d_value = collect_sum(recv_ref, BLOCK) * slope_ref[:, WIDTH:]
    d_gate = d_gated_ref[:BLOCK, :] * att_hat * slope_ref[:, :WIDTH]
    d_query = collect(recv_ref, 2 * BLOCK, QUERIES)
    d_key = collect_sum(recv_ref, 0)
    d_normed = jnp.zeros((BLOCK, WIDTH), F32)
    for k, part in enumerate((d_gate, d_value, d_query, d_key)):
        d_normed += dot_nt(part.astype(BF16), proj_in_ref[:, k * WIDTH : (k + 1) * WIDTH])
    normed, inv_std = normalize(embedded_ref[...].astype(F32))
    d_embedded = upstream_ref[...].astype(F32) + norm_back(d_normed, normed, inv_std)
    d_embedded = jnp.where(valid, d_embedded, 0.0).astype(BF16)
    in_head, in_first, in_second = place_masks(d_gated_ref)
    half = WIDTH // 2
    out_ref[:, :WIDTH] = dot(in_head, d_embedded).astype(BF16)
    out_ref[:, WIDTH:] = (
        dot(in_first, d_embedded[:, :half]) + dot(in_second, d_embedded[:, half:])
    ).astype(BF16)


def scatter_kernel(wanted_ref, arrived_ref, out_ref):
    half = WIDTH // 2
    rest = arrived_ref[:, WIDTH:]
    row = (iota((SHARD_ROWS, SENT), 0) + 1).astype(F32)
    total = dot(one_hot(row == wanted_ref[0:1, :]), arrived_ref[:, :WIDTH])
    for k, start in enumerate((0, half)):
        tail = dot(one_hot(row == wanted_ref[k + 1 : k + 2, :]), rest)
        out_ref[:, start : start + half] = (total[:, start : start + half] + tail).astype(BF16)


def output_kernel(parts_ref, gated_ref, embedded_ref, proj_out_ref, grad_ref, out_ref):
    output = embedded_ref[...].astype(F32) + dot(gated_ref[...], proj_out_ref[...])
    out_ref[...] = output.astype(BF16)
    total = parts_ref[0].astype(F32)
    for k in range(1, GROUPS):
        total += parts_ref[k].astype(F32)
    grad_ref[...] = total


WHOLE = pl.BlockSpec(memory_space=pltpu.VMEM)


def run(kernel, name, outs, *args, scratch=(), vmem=40):
    single = not isinstance(outs, (list, tuple))
    return pl.pallas_call(
        kernel,
        out_shape=outs,
        in_specs=[WHOLE] * len(args),
        out_specs=WHOLE if single else [WHOLE] * len(outs),
        scratch_shapes=scratch,
        compiler_params=pltpu.CompilerParams(vmem_limit_bytes=vmem * 1024 * 1024),
        name=name,
    )(*args)


def shape(*dims, dtype=BF16):
    return jax.ShapeDtypeStruct(dims, dtype)


def swap(array, axis, groups=None):
    return lax.all_to_all(
        array, axis, split_axis=0, concat_axis=0, tiled=True, axis_index_groups=groups
    )


def local(item_ids, history_len, item_slot, table_slab, proj_in, proj_out, upstream):
    upstream = upstream[0]
    order = [[2 * (4 * (3 - (p // 2) % 4) + ((p // 2) // 4 + 3 * ((p // 2) % 4)) % 4) + p % 2 for p in range(TABLES)]]
    requests, info = run(
        index_kernel,
        "index",
        [shape(TABLES, BLOCK, dtype=jnp.int32), shape(8, BLOCK, dtype=jnp.int32)],
        history_len.reshape(1, 1),
        item_ids,
        item_slot.reshape(BLOCK, BLOCK),
        vmem=60,
    )
    asked = swap(requests.reshape(TABLES, 1, BLOCK), "table", order)
    slab, d_gated = run(
        prepare_kernel,
        "prepare",
        [shape(SHARD_ROWS, WIDTH), shape(BLOCK + 8, WIDTH, dtype=F32)],
        table_slab,
        info,
        upstream,
        proj_out,
    )
    rows_out, wanted = run(
        gather_kernel, "gather", [shape(SENT, PACKED), shape(8, SENT, dtype=F32)], asked, slab
    )
    rows = swap(rows_out.reshape(TABLES, MAIN, PACKED), "table", order).reshape(SENT, PACKED)
    send, embedded, gate, slope = run(
        project_kernel,
        "project",
        [
            shape(GROUPS, PIECE, HEAD_DIM),
            shape(BLOCK, WIDTH),
            shape(BLOCK, WIDTH),
            shape(BLOCK, 2 * WIDTH, dtype=F32),
        ],
        rows,
        proj_in,
        d_gated,
    )
    recv = swap(send, "ctx", [ORDER])
    att, d_hat, stats = run(
        attend_kernel,
        "attend",
        [
            shape(HEAD_DIM, SPAN, dtype=F32),
            shape(HEAD_DIM, SPAN, dtype=F32),
            shape(HEADS, 4, SPAN, dtype=F32),
        ],
        recv,
    )
    lines = [[HEADS * g + h for h in range(HEADS)] for g in range(GROUPS // HEADS)]
    stats = swap(stats, "ctx", lines)
    send_back = run(
        backward_kernel,
        "backward",
        shape(GROUPS, PIECE, HEAD_DIM),
        recv,
        att,
        d_hat,
        stats,
        scratch=[pltpu.VMEM((HEAD_DIM, SPAN), F32)],
    )
    back = swap(send_back, "ctx", [ORDER])
    outgoing, gated = run(
        finish_kernel,
        "finish",
        [shape(SENT, PACKED), shape(BLOCK, WIDTH)],
        back,
        embedded,
        gate,
        slope,
        d_gated,
        upstream,
        proj_in,
    )
    arrived = swap(outgoing.reshape(TABLES, MAIN, PACKED), "table", order).reshape(SENT, PACKED)
    sums = run(scatter_kernel, "scatter", shape(SHARD_ROWS, WIDTH), wanted, arrived)
    parts = swap(sums.reshape(GROUPS, SHARD_ROWS // GROUPS, WIDTH), "ctx")
    table_grad, layer_out = run(
        output_kernel,
        "output",
        [shape(SHARD_ROWS // GROUPS, WIDTH, dtype=F32), shape(BLOCK, WIDTH)],
        parts,
        gated,
        embedded,
        proj_out,
    )
    return (layer_out[None], table_grad)


def solution(mesh):
    placed = (
        P("table", "ctx"),
        P("table"),
        P(),
        P("table", None),
        P(),
        P(),
        P("table", "ctx", None),
    )
    return jax.shard_map(
        local,
        mesh=mesh,
        in_specs=placed,
        out_specs=(P("table", "ctx", None), P(("table", "ctx"), None)),
        check_vma=False,
    )
```

```python
import jax
import jax.numpy as jnp
from jax import lax
from jax.experimental import pallas as pl
from jax.experimental.pallas import tpu as pltpu
from jax.sharding import PartitionSpec as P

EPSILON = 1e-05
BLOCK = 128
WIDTH = 512
HEADS = 4
HEAD_DIM = 128
TABLES = 32
GROUPS = 16
SHARD_ROWS = 512
QUERIES = BLOCK // HEADS
SEQ = BLOCK * GROUPS
SPAN = 4 * BLOCK
SCALE = HEAD_DIM ** (-0.5)
PIECE = 2 * BLOCK + 2 * QUERIES
MAIN = 8
SENT = TABLES * MAIN
PACKED = WIDTH + WIDTH // 2
ORDER = [0, 1, 2, 3, 7, 6, 5, 4, 8, 9, 10, 11, 15, 14, 13, 12]
PLACE = [ORDER.index(c) for c in range(GROUPS)]

F32 = jnp.float32
BF16 = jnp.bfloat16


def dot(a, b):
    return jnp.dot(a, b, preferred_element_type=F32)


def dot_nt(a, b):
    return lax.dot_general(a, b, (((1,), (1,)), ((), ())), preferred_element_type=F32)


def dot_tn(a, b):
    return lax.dot_general(a, b, (((0,), (0,)), ((), ())), preferred_element_type=F32)


def iota(shape, dim):
    return lax.broadcasted_iota(jnp.int32, shape, dim)


def one_hot(mask):
    return jnp.where(mask, 1.0, 0.0).astype(BF16)


def normalize(values):
    centre = values - jnp.mean(values, axis=-1, keepdims=True)
    scale_inv = lax.rsqrt(jnp.mean(centre * centre, axis=-1, keepdims=True) + EPSILON)
    return (centre * scale_inv, scale_inv)


def silu_and_slope(values):
    half = 0.5 * values
    th = jnp.tanh(half)
    out = half + half * th
    return out, 0.5 * ((1.0 + th) + out * (1.0 - th))


def norm_back(grad, normed, scale_inv):
    return scale_inv * (
        grad
        - jnp.mean(grad, axis=-1, keepdims=True)
        - normed * jnp.mean(grad * normed, axis=-1, keepdims=True)
    )


def index_kernel(length_ref, ids_ref, slot_ref, send_ref, info_ref):
    ids = ids_ref[...]
    event = iota((1, BLOCK), 1)
    length = length_ref[...]
    valid = lax.axis_index("ctx") * BLOCK + event < length
    row = iota((BLOCK, BLOCK), 0)
    table = slot_ref[...]
    rows_hot = one_hot(row == (ids >> 7))
    high = dot_tn((table >> 7).astype(F32).astype(BF16), rows_hot)
    low = dot_tn((table & 127).astype(F32).astype(BF16), rows_hot)
    both = jnp.where(row == (ids & 127), high * 128.0 + low, 0.0)
    slots = jnp.sum(both, axis=0, keepdims=True).astype(jnp.int32)
    shard = slots >> 9
    turn = 4 * ((((shard >> 1) & 3) - 3 * (3 - ((shard >> 1) >> 2))) & 3) + 3 - ((shard >> 1) >> 2)
    owner = jnp.where(valid, 2 * turn + ((shard + turn) & 1), TABLES)
    wanted = (slots & (SHARD_ROWS - 1)) + 1
    owned = iota((TABLES, BLOCK), 0) == owner
    owned_hot = one_hot(owned)
    earlier = dot(owned_hot, one_hot(row < iota((BLOCK, BLOCK), 1)))
    rank = jnp.sum(jnp.where(owned, earlier, 0.0), axis=0, keepdims=True).astype(jnp.int32)
    head = jnp.where(valid & (rank < MAIN), owner * MAIN + rank, -1000)
    tail = jnp.where(valid & (rank >= MAIN), owner * MAIN + rank - MAIN, -1000)
    lengths = jnp.broadcast_to(length, (6, BLOCK))
    info_ref[...] = jnp.concatenate([head, tail, lengths], axis=0)
    ranked = jnp.where(row < BLOCK // 2, row & 7, MAIN + (row & 3)) == rank
    wanted_high = jnp.where(ranked, (wanted >> 5).astype(F32), 0.0).astype(BF16)
    wanted_low = jnp.where(ranked, (wanted & 31).astype(F32), 0.0).astype(BF16)
    asked = dot_nt(owned_hot, wanted_high) * 32.0 + dot_nt(owned_hot, wanted_low)
    send_ref[...] = asked.astype(jnp.int32)


def asked_rows(asked_ref):
    asked = asked_ref[...].reshape(TABLES, BLOCK).astype(F32)
    turned = pltpu.roll(asked, BLOCK // 2, 1)
    left = iota((TABLES, BLOCK), 1) < BLOCK // 2
    both = []
    for wanted in (jnp.where(left, asked, turned), jnp.where(left, turned, asked)):
        parts = []
        for k in range(SENT // BLOCK):
            own = iota((TABLES, BLOCK), 0) == (iota((TABLES, BLOCK), 1) >> 3) + k * BLOCK // MAIN
            parts.append(jnp.sum(jnp.where(own, wanted, 0.0), axis=0, keepdims=True))
        both.append(jnp.concatenate(parts, axis=1))
    return both


def gather_kernel(asked_ref, slab_ref, out_ref, rows_ref):
    head, tail = asked_rows(asked_ref)
    first = (iota((1, SENT), 1) & 7) < 4
    tail_first = jnp.where(first, tail, 0.0)
    tail_second = jnp.where(first, 0.0, tail)
    rows_ref[...] = jnp.concatenate(
        [head, tail_first, tail_second, head, tail_first, tail_second, head, tail], axis=0
    )
    half = WIDTH // 2
    row = (iota((SHARD_ROWS, SENT), 0) + 1).astype(F32)
    out_ref[:, :WIDTH] = dot_tn(one_hot(row == head), slab_ref[...]).astype(BF16)
    rest = dot_tn(one_hot(row == tail_first), slab_ref[:, :half])
    rest += dot_tn(one_hot(row == tail_second), slab_ref[:, half:])
    out_ref[:, WIDTH:] = rest.astype(BF16)


def valid_rows(d_gated_ref):
    length = d_gated_ref[BLOCK + 2 : BLOCK + 3, 0:1].astype(jnp.int32)
    return lax.axis_index("ctx") * BLOCK + iota((BLOCK, WIDTH), 0) < length


def place_masks(d_gated_ref):
    place = iota((SENT, BLOCK), 0)
    head = d_gated_ref[BLOCK : BLOCK + 1, :BLOCK].astype(jnp.int32)
    tail = d_gated_ref[BLOCK + 1 : BLOCK + 2, :BLOCK].astype(jnp.int32)
    return one_hot(place == head), one_hot(place == tail), one_hot(place == tail + 4)


def prepare_kernel(slab_ref, info_ref, upstream_ref, proj_out_ref, narrow_ref, d_gated_ref):
    narrow_ref[...] = slab_ref[...].astype(BF16)
    place = lax.axis_index("ctx") * BLOCK + iota((BLOCK, WIDTH), 0)
    d_out = jnp.where(place < info_ref[2:3, 0:1], upstream_ref[...], jnp.zeros((), BF16))
    d_gated_ref[:BLOCK, :] = dot_nt(d_out, proj_out_ref[...])
    d_gated_ref[BLOCK:, :BLOCK] = info_ref[...].astype(F32)
    d_gated_ref[BLOCK:, BLOCK:] = jnp.zeros((8, WIDTH - BLOCK), F32)


def project_kernel(
    rows_ref, proj_in_ref, d_gated_ref, send_ref, embedded_ref, gate_ref, slope_ref
):
    in_head, in_first, in_second = place_masks(d_gated_ref)
    half = WIDTH // 2
    rest = rows_ref[:, WIDTH:]
    embedded = dot_tn(in_head, rows_ref[:, :WIDTH]) + jnp.concatenate(
        [dot_tn(in_first, rest), dot_tn(in_second, rest)], axis=1
    )
    valid = valid_rows(d_gated_ref)
    embedded = jnp.where(valid, embedded, 0.0)
    embedded_ref[...] = embedded.astype(BF16)
    normed = normalize(embedded)[0].astype(BF16)

    def part(k):
        return dot(normed, proj_in_ref[:, k * WIDTH : (k + 1) * WIDTH])

    gate_part = part(0)
    value_part = part(1)
    gate, slope_ref[:, :WIDTH] = silu_and_slope(gate_part)
    value, slope_ref[:, WIDTH:] = silu_and_slope(value_part)
    gate, value = gate.astype(BF16), value.astype(BF16)
    gate_ref[...] = gate
    value = jnp.where(valid, value, jnp.zeros((), BF16))
    query = part(2).astype(BF16)
    key = jnp.where(valid, part(3), 0.0).astype(BF16)
    d_hat = (d_gated_ref[:BLOCK, :] * gate.astype(F32)).astype(BF16)
    for h in range(HEADS):
        cols = slice(h * HEAD_DIM, (h + 1) * HEAD_DIM)
        for g in range(HEADS):
            rows = slice(g * QUERIES, (g + 1) * QUERIES)
            chunk = PLACE[HEADS * g + h]
            send_ref[chunk, 0:BLOCK, :] = key[:, cols]
            send_ref[chunk, BLOCK : 2 * BLOCK, :] = value[:, cols]
            send_ref[chunk, 2 * BLOCK : 2 * BLOCK + QUERIES, :] = query[rows, cols]
            send_ref[chunk, 2 * BLOCK + QUERIES :, :] = d_hat[rows, cols]


def allowed_mask():
    group = lax.axis_index("ctx") // HEADS
    lane = iota((SPAN, BLOCK), 1)
    place = (lane // QUERIES) * BLOCK + group * QUERIES + lane % QUERIES
    return iota((SPAN, BLOCK), 0) <= place


def take(recv_ref, blocks, first, rows):
    return jnp.concatenate([recv_ref[PLACE[c], first : first + rows, :] for c in blocks], axis=0)


def span_keys(recv_ref, j):
    blocks = range(4 * j, 4 * j + 4)
    return take(recv_ref, blocks, 0, BLOCK), take(recv_ref, blocks, BLOCK, BLOCK)


def attend_kernel(recv_ref, att_ref, d_hat_ref, stats_ref):
    query = take(recv_ref, range(GROUPS), 2 * BLOCK, QUERIES)
    mask = allowed_mask()
    for j in range(4):
        key, value = span_keys(recv_ref, j)
        start = j * BLOCK
        parts = []
        for k in range(0, SPAN, SPAN // 2):
            rows = slice(k, k + SPAN // 2)
            half = dot_nt(key[rows], query[start:, :]) * (0.5 * SCALE)
            weight = half + half * jnp.tanh(half)
            first = jnp.where(mask[rows], weight[:, :BLOCK], 0.0)
            if j < 3:
                first = jnp.concatenate([first, weight[:, BLOCK:]], axis=1)
            parts.append(first.astype(BF16))
        part = dot_tn(value, jnp.concatenate(parts, axis=0))
        if j == 0:
            att_ref[...] = part
        else:
            att_ref[:, start:] += part
    d_hat = take(recv_ref, range(GROUPS), 2 * BLOCK + QUERIES, QUERIES)
    d_hat = d_hat.astype(F32).T
    d_hat_ref[...] = d_hat
    att = att_ref[...]
    mean = jnp.mean(att, axis=0, keepdims=True)
    centre = att - mean
    d_mean = jnp.mean(d_hat, axis=0, keepdims=True)
    spread_sum = jnp.sum(centre * centre, axis=0, keepdims=True)
    cross_sum = jnp.sum(centre * (d_hat - d_mean), axis=0, keepdims=True)
    rows = jnp.concatenate([mean, spread_sum, d_mean, cross_sum], axis=0)
    for k in range(HEADS):
        stats_ref[k] = rows


def backward_kernel(recv_ref, att_ref, d_hat_ref, stats_ref, send_ref, d_query_ref):
    query = take(recv_ref, range(GROUPS), 2 * BLOCK, QUERIES)
    mask = allowed_mask()
    stats = [stats_ref[k] for k in range(HEADS)]

    def average(row):
        return sum(s[row : row + 1, :] for s in stats) / HEADS

    mean, d_mean = average(0), average(2)
    spread_mean = average(1) / HEAD_DIM + sum(
        (s[0:1, :] - mean) * (s[0:1, :] - mean) for s in stats
    ) / HEADS
    cross_mean = average(3) / HEAD_DIM + sum(
        (s[0:1, :] - mean) * (s[2:3, :] - d_mean) for s in stats
    ) / HEADS
    inv = lax.rsqrt(spread_mean + EPSILON)
    att = att_ref[...]
    att_hat = (att - mean) * inv
    d_att = (inv * (d_hat_ref[...] - d_mean - att_hat * (inv * cross_mean))).astype(BF16)
    out_att = att.T.astype(BF16)
    for j in range(4):
        key, value = span_keys(recv_ref, j)
        start = j * BLOCK
        half = dot_nt(key, query[start:, :]) * (0.5 * SCALE)
        th = jnp.tanh(half)
        weight = half + half * th
        slope = (0.5 * SCALE) * ((1.0 + th) + weight * (1.0 - th))
        d_score = dot(value, d_att[:, start:]) * slope

        def masked(values):
            first = jnp.where(mask, values[:, :BLOCK], 0.0)
            if j == 3:
                return first.astype(BF16)
            return jnp.concatenate([first, values[:, BLOCK:]], axis=1).astype(BF16)

        weight, d_score = masked(weight), masked(d_score)
        d_key = dot(d_score, query[start:, :]).astype(BF16)
        d_value = dot_nt(weight, d_att[:, start:]).astype(BF16)
        part = dot_tn(key, d_score)
        if j == 0:
            d_query_ref[...] = part
        else:
            d_query_ref[:, start:] += part
        for k in range(4):
            rows = slice(k * BLOCK, (k + 1) * BLOCK)
            send_ref[PLACE[4 * j + k], 0:BLOCK, :] = d_key[rows]
            send_ref[PLACE[4 * j + k], BLOCK : 2 * BLOCK, :] = d_value[rows]
    d_query = d_query_ref[...].T.astype(BF16)
    for c in range(GROUPS):
        rows = slice(c * QUERIES, (c + 1) * QUERIES)
        send_ref[PLACE[c], 2 * BLOCK : 2 * BLOCK + QUERIES, :] = d_query[rows]
        send_ref[PLACE[c], 2 * BLOCK + QUERIES :, :] = out_att[rows]


def collect(recv_ref, first, rows):
    return jnp.concatenate(
        [
            jnp.concatenate([recv_ref[PLACE[HEADS * g + h], first : first + rows, :] for g in range(HEADS)], axis=0)
            for h in range(HEADS)
        ],
        axis=1,
    ).astype(F32)


def collect_sum(recv_ref, first):
    def head(h):
        return sum(
            recv_ref[PLACE[HEADS * g + h], first : first + BLOCK, :].astype(F32) for g in range(HEADS)
        )

    return jnp.concatenate([head(h) for h in range(HEADS)], axis=1)


def finish_kernel(
    recv_ref,
    embedded_ref,
    gate_ref,
    slope_ref,
    d_gated_ref,
    upstream_ref,
    proj_in_ref,
    out_ref,
    gated_ref,
):
    att_hat = normalize(collect(recv_ref, 2 * BLOCK + QUERIES, QUERIES))[0]
    valid = valid_rows(d_gated_ref)
    gated_ref[...] = jnp.where(valid, att_hat * gate_ref[...].astype(F32), 0.0).astype(BF16)
    d_value = collect_sum(recv_ref, BLOCK) * slope_ref[:, WIDTH:]
    d_gate = d_gated_ref[:BLOCK, :] * att_hat * slope_ref[:, :WIDTH]
    d_query = collect(recv_ref, 2 * BLOCK, QUERIES)
    d_key = collect_sum(recv_ref, 0)
    d_normed = jnp.zeros((BLOCK, WIDTH), F32)
    for k, part in enumerate((d_gate, d_value, d_query, d_key)):
        d_normed += dot_nt(part.astype(BF16), proj_in_ref[:, k * WIDTH : (k + 1) * WIDTH])
    normed, inv_std = normalize(embedded_ref[...].astype(F32))
    d_embedded = upstream_ref[...].astype(F32) + norm_back(d_normed, normed, inv_std)
    d_embedded = jnp.where(valid, d_embedded, 0.0).astype(BF16)
    in_head, in_first, in_second = place_masks(d_gated_ref)
    half = WIDTH // 2
    out_ref[:, :WIDTH] = dot(in_head, d_embedded).astype(BF16)
    out_ref[:, WIDTH:] = (
        dot(in_first, d_embedded[:, :half]) + dot(in_second, d_embedded[:, half:])
    ).astype(BF16)


def scatter_kernel(wanted_ref, arrived_ref, out_ref):
    half = WIDTH // 2
    rest = arrived_ref[:, WIDTH:]
    row = (iota((SHARD_ROWS, SENT), 0) + 1).astype(F32)
    total = dot(one_hot(row == wanted_ref[0:1, :]), arrived_ref[:, :WIDTH])
    for k, start in enumerate((0, half)):
        tail = dot(one_hot(row == wanted_ref[k + 1 : k + 2, :]), rest)
        out_ref[:, start : start + half] = (total[:, start : start + half] + tail).astype(BF16)


def output_kernel(parts_ref, gated_ref, embedded_ref, proj_out_ref, grad_ref, out_ref):
    output = embedded_ref[...].astype(F32) + dot(gated_ref[...], proj_out_ref[...])
    out_ref[...] = output.astype(BF16)
    total = parts_ref[0].astype(F32)
    for k in range(1, GROUPS):
        total += parts_ref[k].astype(F32)
    grad_ref[...] = total


WHOLE = pl.BlockSpec(memory_space=pltpu.VMEM)


def run(kernel, name, outs, *args, scratch=(), vmem=40):
    single = not isinstance(outs, (list, tuple))
    return pl.pallas_call(
        kernel,
        out_shape=outs,
        in_specs=[WHOLE] * len(args),
        out_specs=WHOLE if single else [WHOLE] * len(outs),
        scratch_shapes=scratch,
        compiler_params=pltpu.CompilerParams(vmem_limit_bytes=vmem * 1024 * 1024),
        name=name,
    )(*args)


def shape(*dims, dtype=BF16):
    return jax.ShapeDtypeStruct(dims, dtype)


def swap(array, axis, groups=None):
    return lax.all_to_all(
        array, axis, split_axis=0, concat_axis=0, tiled=True, axis_index_groups=groups
    )


def local(item_ids, history_len, item_slot, table_slab, proj_in, proj_out, upstream):
    upstream = upstream[0]
    order = [[2 * (4 * (3 - (p // 2) % 4) + ((p // 2) // 4 + 3 * ((p // 2) % 4)) % 4) + (p + p // 2) % 2 for p in range(TABLES)]]
    requests, info = run(
        index_kernel,
        "index",
        [shape(TABLES, BLOCK, dtype=jnp.int32), shape(8, BLOCK, dtype=jnp.int32)],
        history_len.reshape(1, 1),
        item_ids,
        item_slot.reshape(BLOCK, BLOCK),
        vmem=60,
    )
    asked = swap(requests.reshape(TABLES, 1, BLOCK), "table", order)
    slab, d_gated = run(
        prepare_kernel,
        "prepare",
        [shape(SHARD_ROWS, WIDTH), shape(BLOCK + 8, WIDTH, dtype=F32)],
        table_slab,
        info,
        upstream,
        proj_out,
    )
    rows_out, wanted = run(
        gather_kernel, "gather", [shape(SENT, PACKED), shape(8, SENT, dtype=F32)], asked, slab
    )
    rows = swap(rows_out.reshape(TABLES, MAIN, PACKED), "table", order).reshape(SENT, PACKED)
    send, embedded, gate, slope = run(
        project_kernel,
        "project",
        [
            shape(GROUPS, PIECE, HEAD_DIM),
            shape(BLOCK, WIDTH),
            shape(BLOCK, WIDTH),
            shape(BLOCK, 2 * WIDTH, dtype=F32),
        ],
        rows,
        proj_in,
        d_gated,
    )
    recv = swap(send, "ctx", [ORDER])
    att, d_hat, stats = run(
        attend_kernel,
        "attend",
        [
            shape(HEAD_DIM, SPAN, dtype=F32),
            shape(HEAD_DIM, SPAN, dtype=F32),
            shape(HEADS, 4, SPAN, dtype=F32),
        ],
        recv,
    )
    lines = [[HEADS * g + h for h in range(HEADS)] for g in range(GROUPS // HEADS)]
    stats = swap(stats, "ctx", lines)
    send_back = run(
        backward_kernel,
        "backward",
        shape(GROUPS, PIECE, HEAD_DIM),
        recv,
        att,
        d_hat,
        stats,
        scratch=[pltpu.VMEM((HEAD_DIM, SPAN), F32)],
    )
    back = swap(send_back, "ctx", [ORDER])
    outgoing, gated = run(
        finish_kernel,
        "finish",
        [shape(SENT, PACKED), shape(BLOCK, WIDTH)],
        back,
        embedded,
        gate,
        slope,
        d_gated,
        upstream,
        proj_in,
    )
    arrived = swap(outgoing.reshape(TABLES, MAIN, PACKED), "table", order).reshape(SENT, PACKED)
    sums = run(scatter_kernel, "scatter", shape(SHARD_ROWS, WIDTH), wanted, arrived)
    parts = swap(sums.reshape(GROUPS, SHARD_ROWS // GROUPS, WIDTH), "ctx")
    table_grad, layer_out = run(
        output_kernel,
        "output",
        [shape(SHARD_ROWS // GROUPS, WIDTH, dtype=F32), shape(BLOCK, WIDTH)],
        parts,
        gated,
        embedded,
        proj_out,
    )
    return (layer_out[None], table_grad)


def solution(mesh):
    placed = (
        P("table", "ctx"),
        P("table"),
        P(),
        P("table", None),
        P(),
        P(),
        P("table", "ctx", None),
    )
    return jax.shard_map(
        local,
        mesh=mesh,
        in_specs=placed,
        out_specs=(P("table", "ctx", None), P(("table", "ctx"), None)),
        check_vma=False,
    )
```
